32 devices in a mesh: rep: 16 (over z, y, core), shard: 2 (over x).
Axes of the slice: x: 2, y: 2, z: 4, core: 2. Of those that a mesh axis runs over, the one named last changes fastest.
Arguments:
- tokens: bfloat16 [4096, 576], P(('rep', 'shard')), may hold values from -6 to 6
- block_order: int32 [16, 2], P('rep'), may hold values from 0 to 1, each once within a row
- attn_gain: bfloat16 [1, 576], P(None, 'shard'), may hold values from 0.5 to 1.5
- q_weight: bfloat16 [1, 576, 576], P(None, 'shard'), may hold values from -0.25 to 0.25
- k_weight: bfloat16 [1, 576, 192], P(None, 'shard'), may hold values from -0.25 to 0.25
- v_weight: bfloat16 [1, 576, 192], P(None, 'shard'), may hold values from -0.25 to 0.25
- o_weight: bfloat16 [1, 576, 576], P(None, 'shard'), may hold values from -3 to 3
- ffn_gain: bfloat16 [1, 576], P(None, 'shard'), may hold values from 0.5 to 1.5
- gate_weight: bfloat16 [1, 576, 1536], P(None, 'shard'), may hold values from -0.25 to 0.25
- up_weight: bfloat16 [1, 576, 1536], P(None, 'shard'), may hold values from -0.25 to 0.25
- down_weight: bfloat16 [1, 1536, 576], P(None, 'shard'), may hold values from -0.15625 to 0.15625
- cotangent: bfloat16 [4096, 576], P(('rep', 'shard')), may hold values from -6 to 6
Outputs:
- block_out: float32 [4096, 576], P(('rep', 'shard'))
- input_grad: float32 [4096, 576], P(('rep', 'shard'))
- grad_attn_gain: float32 [1, 576], P(None, 'shard')
- grad_q_weight: float32 [1, 576, 576], P(None, 'shard')
- grad_k_weight: float32 [1, 576, 192], P(None, 'shard')
- grad_v_weight: float32 [1, 576, 192], P(None, 'shard')
- grad_o_weight: float32 [1, 576, 576], P(None, 'shard')
- grad_ffn_gain: float32 [1, 576], P(None, 'shard')
- grad_gate_weight: float32 [1, 576, 1536], P(None, 'shard')
- grad_up_weight: float32 [1, 576, 1536], P(None, 'shard')
- grad_down_weight: float32 [1, 1536, 576], P(None, 'shard')
The draws below stay inside these ranges and needn't reach their ends.
Inputs may be any that keep to these rules, and one draw needn't show every extreme that they name: `block_order`: each row lists every number 0 to 1 once.
All inputs are finite; a program needn't handle non-finite values.
Results may differ from the reference program's by a relative error of at most 0.012.
Values may be sent and summed in bfloat16 or wider, within the bound.
A program may use at most 128 MiB of HBM per device.

```python
import math
import jax
import jax.numpy as jnp
from jax import lax

D = 576
H = 9
KV = 3
HD = 64
FF = 1536
LAYERS = 1
TOK_DEV = 128
SEQS = 16
TOKENS = 4096
N_SHARD = 2


def block_scale(stream_key, extent, pieces, least, largest):
    def one(position, blocks):
        heights = jax.random.uniform(jax.random.fold_in(jax.random.fold_in(stream_key, 6), position), (blocks,), jnp.float32, least / len(pieces), largest / len(pieces))
        return jnp.repeat(jnp.exp(heights), extent[position] // blocks).reshape((-1,) + (1,) * (len(extent) - position - 1))

    factor_of = one(*pieces[0])
    for cut in pieces[1:]:
        factor_of = factor_of * one(*cut)
    return factor_of


def bell_draw(key, extent, width, bound, split=(), held_as=jnp.bfloat16):
    gain = block_scale(key, extent, split, -0.22, 0.18) if split else 1.0
    values = jax.random.normal(key, extent, jnp.float32) * width * gain
    return jnp.minimum(jnp.maximum(values, -bound), bound).astype(held_as)


def setup_inputs(seed: int = 0) -> dict:
    streams_of = jax.random.split(jax.random.key(seed), 13)
    tokens = bell_draw(streams_of[0], (TOKENS, D), 1.0, 6.0, ((0, 32),))
    block_order = jax.vmap(lambda own: jax.random.permutation(own, N_SHARD))(jax.random.split(streams_of[1], SEQS)).reshape((SEQS, N_SHARD)).astype(jnp.int32)
    attn_gain = jnp.clip(1.0 + 0.1 * jax.random.normal(streams_of[2], (LAYERS, D), jnp.float32), 0.5, 1.5).astype(jnp.bfloat16)
    q_weight = bell_draw(streams_of[3], (LAYERS, D, H * HD), D ** -0.5, 0.25, ((1, 2),))
    k_weight = bell_draw(streams_of[4], (LAYERS, D, KV * HD), D ** -0.5, 0.25, ((1, 2),))
    v_weight = bell_draw(streams_of[5], (LAYERS, D, KV * HD), D ** -0.5, 0.25, ((1, 2),))
    o_weight = bell_draw(streams_of[6], (LAYERS, H * HD, D), 4 ** -0.5, 3.0, ((1, 2),))
    ffn_gain = jnp.clip(1.0 + 0.1 * jax.random.normal(streams_of[7], (LAYERS, D), jnp.float32), 0.5, 1.5).astype(jnp.bfloat16)
    gate_weight = bell_draw(streams_of[8], (LAYERS, D, FF), D ** -0.5, 0.25, ((1, 2),))
    up_weight = bell_draw(streams_of[9], (LAYERS, D, FF), D ** -0.5, 0.25, ((1, 2),))
    down_weight = bell_draw(streams_of[10], (LAYERS, FF, D), FF ** -0.5, 0.15625, ((1, 2),))
    cotangent = bell_draw(streams_of[11], (TOKENS, D), 1.0, 6.0, ((0, 32),))
    return {"tokens": tokens, "block_order": block_order, "attn_gain": attn_gain, "q_weight": q_weight, "k_weight": k_weight, "v_weight": v_weight, "o_weight": o_weight, "ffn_gain": ffn_gain, "gate_weight": gate_weight, "up_weight": up_weight, "down_weight": down_weight, "cotangent": cotangent}


rope_base = 100000.0
norm_eps = 1e-05

def rope_tables(positions):
    half_dim = HD // 2
    frequency = jnp.exp(jnp.arange(half_dim, dtype=jnp.float32) * (-2.0 * math.log(rope_base) / HD))
    angles = positions.astype(jnp.float32)[:, None] * frequency[None, :]
    return (jnp.cos(angles)[:, None, :], jnp.sin(angles)[:, None, :])

def rotate(tensor, cos_table, sin_table):
    half_dim = tensor.shape[-1] // 2
    first_half = tensor[..., :half_dim]
    second_half = tensor[..., half_dim:]
    return jnp.concatenate([first_half * cos_table - second_half * sin_table, second_half * cos_table + first_half * sin_table], axis=-1)

def rotate_back(tensor, cos_table, sin_table):
    half_dim = tensor.shape[-1] // 2
    first_half = tensor[..., :half_dim]
    second_half = tensor[..., half_dim:]
    return jnp.concatenate([first_half * cos_table + second_half * sin_table, second_half * cos_table - first_half * sin_table], axis=-1)

def rms_scale(hidden):
    factor = lax.rsqrt(lax.optimization_barrier(jnp.mean(hidden * hidden, axis=-1, keepdims=True)) + norm_eps)
    return (hidden * factor, factor)

def rms_back(grad_in, normed, factor, gain_row):
    scaled = grad_in * gain_row.astype(jnp.float32)
    return factor * (scaled - normed * lax.optimization_barrier(jnp.mean(scaled * normed, axis=-1, keepdims=True)))

def visible_scores(query_rows, key_rows, q_positions, k_positions):
    scores = jnp.einsum('sgmd,tgd->gmst', query_rows.astype(jnp.float32), key_rows.astype(jnp.float32)) * HD ** (-0.5)
    allowed = k_positions[None, :] <= q_positions[:, None]
    return (jnp.where(allowed, scores, -1e+30), allowed)

def layer_forward(hidden, weights, positions, cos_table, sin_table):
    attn_g, q_w, k_w, v_w, o_w, ffn_g, gate_w, up_w, down_w = weights
    row_count = hidden.shape[0]
    head_groups = H // KV
    normed, factor = rms_scale(hidden)
    attn_in = (normed * attn_g.astype(jnp.float32)).astype(jnp.bfloat16)
    query_rows = rotate(jnp.dot(attn_in, q_w, preferred_element_type=jnp.float32).reshape(row_count, H, HD), cos_table, sin_table).astype(jnp.bfloat16)
    key_rows = rotate(jnp.dot(attn_in, k_w, preferred_element_type=jnp.float32).reshape(row_count, KV, HD), cos_table, sin_table).astype(jnp.bfloat16)
    value_rows = jnp.dot(attn_in, v_w, preferred_element_type=jnp.float32).astype(jnp.bfloat16).reshape(row_count, KV, HD)
    query_grouped = query_rows.reshape(row_count, KV, head_groups, HD)
    scores, allowed = visible_scores(query_grouped, key_rows, positions, positions)
    row_max = lax.optimization_barrier(jnp.max(scores, axis=-1, keepdims=True))
    exponent = jnp.exp(scores - row_max)
    row_total = lax.optimization_barrier(jnp.sum(exponent, axis=-1, keepdims=True))
    log_total = (row_max + jnp.log(row_total))[..., 0]
    probs_bf = jnp.where(allowed, jnp.exp(scores - log_total[..., None]), 0.0).astype(jnp.bfloat16)
    attended = jnp.einsum('gmst,tgd->sgmd', probs_bf.astype(jnp.float32), value_rows.astype(jnp.float32)).astype(jnp.bfloat16).reshape(row_count, H * HD)
    middle = hidden + jnp.dot(attended, o_w, preferred_element_type=jnp.float32)
    normed_two, factor_two = rms_scale(middle)
    ffn_in = (normed_two * ffn_g.astype(jnp.float32)).astype(jnp.bfloat16)
    gate_pre = jnp.dot(ffn_in, gate_w, preferred_element_type=jnp.float32)
    up_pre = jnp.dot(ffn_in, up_w, preferred_element_type=jnp.float32)
    mixed = (jax.nn.silu(gate_pre) * up_pre).astype(jnp.bfloat16)
    output = middle + jnp.dot(mixed, down_w, preferred_element_type=jnp.float32)
    saved = (normed, factor, attn_in, query_rows, key_rows, value_rows, log_total, attended, normed_two, factor_two, ffn_in, gate_pre, up_pre, mixed)
    return (output, saved)

def layer_backward(gradient, saved, weights, positions, cos_table, sin_table):
    attn_g, q_w, k_w, v_w, o_w, ffn_g, gate_w, up_w, down_w = weights
    normed, factor, attn_in, query_rows, key_rows, value_rows, log_total, attended, normed_two, factor_two, ffn_in, gate_pre, up_pre, mixed = saved
    row_count = gradient.shape[0]
    head_groups = H // KV
    grad_bf = gradient.astype(jnp.bfloat16)
    g_down = jnp.dot(mixed.T, grad_bf, preferred_element_type=jnp.float32)
    g_mixed = jnp.dot(grad_bf, down_w.T, preferred_element_type=jnp.float32)
    sigmoid_gate = jax.nn.sigmoid(gate_pre)
    g_up = (g_mixed * gate_pre * sigmoid_gate).astype(jnp.bfloat16)
    g_gate = (g_mixed * up_pre * sigmoid_gate * (1.0 + gate_pre * (1.0 - sigmoid_gate))).astype(jnp.bfloat16)
    g_gate_w = jnp.dot(ffn_in.T, g_gate, preferred_element_type=jnp.float32)
    g_up_w = jnp.dot(ffn_in.T, g_up, preferred_element_type=jnp.float32)
    g_ffn_in = jnp.dot(g_gate, gate_w.T, preferred_element_type=jnp.float32) + jnp.dot(g_up, up_w.T, preferred_element_type=jnp.float32)
    g_ffn_gain = lax.optimization_barrier(jnp.sum(g_ffn_in * normed_two, axis=0))
    g_middle = gradient + rms_back(g_ffn_in, normed_two, factor_two, ffn_g)
    middle_bf = g_middle.astype(jnp.bfloat16)
    g_o_w = jnp.dot(attended.T, middle_bf, preferred_element_type=jnp.float32)
    g_attended = jnp.dot(middle_bf, o_w.T, preferred_element_type=jnp.float32).astype(jnp.bfloat16).reshape(row_count, KV, head_groups, HD)
    query_grouped = query_rows.reshape(row_count, KV, head_groups, HD)
    scores, allowed = visible_scores(query_grouped, key_rows, positions, positions)
    probs = jnp.where(allowed, jnp.exp(scores - log_total[..., None]), 0.0)
    probs_bf = probs.astype(jnp.bfloat16)
    value_terms = jnp.einsum('gmst,sgmd->tgd', probs_bf.astype(jnp.float32), g_attended.astype(jnp.float32))
    g_probs = jnp.einsum('sgmd,tgd->gmst', g_attended.astype(jnp.float32), value_rows.astype(jnp.float32))
    delta = jnp.einsum('sgmd,sgmd->gms', g_attended.astype(jnp.float32), attended.reshape(row_count, KV, head_groups, HD).astype(jnp.float32))
    g_scores = (probs * (g_probs - delta[..., None]) * HD ** (-0.5)).astype(jnp.bfloat16)
    g_query = jnp.einsum('gmst,tgd->sgmd', g_scores.astype(jnp.float32), key_rows.astype(jnp.float32))
    key_terms = jnp.einsum('gmst,sgmd->tgd', g_scores.astype(jnp.float32), query_grouped.astype(jnp.float32))
    g_query_bf = rotate_back(g_query.reshape(row_count, H, HD), cos_table, sin_table).reshape(row_count, H * HD).astype(jnp.bfloat16)
    g_key_bf = rotate_back(key_terms, cos_table, sin_table).reshape(row_count, KV * HD).astype(jnp.bfloat16)
    g_value_bf = value_terms.reshape(row_count, KV * HD).astype(jnp.bfloat16)
    g_q_w = jnp.dot(attn_in.T, g_query_bf, preferred_element_type=jnp.float32)
    g_k_w = jnp.dot(attn_in.T, g_key_bf, preferred_element_type=jnp.float32)
    g_v_w = jnp.dot(attn_in.T, g_value_bf, preferred_element_type=jnp.float32)
    g_attn_in = jnp.dot(g_query_bf, q_w.T, preferred_element_type=jnp.float32) + jnp.dot(g_key_bf, k_w.T, preferred_element_type=jnp.float32) + jnp.dot(g_value_bf, v_w.T, preferred_element_type=jnp.float32)
    g_attn_gain = lax.optimization_barrier(jnp.sum(g_attn_in * normed, axis=0))
    g_hidden = g_middle + rms_back(g_attn_in, normed, factor, attn_g)
    terms = (g_attn_gain, g_q_w, g_k_w, g_v_w, g_o_w, g_ffn_gain, g_gate_w, g_up_w, g_down)
    return (g_hidden, terms)

def reference(tokens, block_order, attn_gain, q_weight, k_weight, v_weight, o_weight, ffn_gain, gate_weight, up_weight, down_weight, cotangent):
    params = (attn_gain, q_weight, k_weight, v_weight, o_weight, ffn_gain, gate_weight, up_weight, down_weight)
    seq_rows = TOK_DEV * N_SHARD

    def one_sequence(accum, inputs):
        token_rows, order_row, cot_rows = inputs
        positions = (order_row[:, None].astype(jnp.int32) * TOK_DEV + jnp.arange(TOK_DEV, dtype=jnp.int32)[None, :]).reshape(-1)
        cos_table, sin_table = rope_tables(positions)
        hidden = token_rows.astype(jnp.float32)
        saved_list = []
        for layer_index in range(LAYERS):
            weights = tuple((param[layer_index] for param in params))
            hidden, saved = layer_forward(hidden, weights, positions, cos_table, sin_table)
            saved_list.append(saved)
        result = hidden
        gradient = cot_rows.astype(jnp.float32)
        for layer_index in reversed(range(LAYERS)):
            weights = tuple((param[layer_index] for param in params))
            gradient, terms = layer_backward(gradient, saved_list[layer_index], weights, positions, cos_table, sin_table)
            accum = tuple((total.at[layer_index].add(term) for total, term in zip(accum, terms)))
        return (accum, (result, gradient))
    init = tuple((jnp.zeros(param.shape, jnp.float32) for param in params))
    inputs = (tokens.reshape(SEQS, seq_rows, D), block_order, cotangent.reshape(SEQS, seq_rows, D))
    accum, (results, gradients) = lax.scan(one_sequence, init, inputs)
    return (results.reshape(TOKENS, D), gradients.reshape(TOKENS, D), accum[0], accum[1], accum[2], accum[3], accum[4], accum[5], accum[6], accum[7], accum[8])
```

```python
import math

import jax
import jax.numpy as jnp
from jax import lax
from jax.experimental import pallas as pl
from jax.experimental.pallas import tpu as pltpu
from jax.sharding import PartitionSpec as P

H = 9
KV = 3
HD = 64
LAYERS = 1


rope_base = 100000.0
norm_eps = 1e-05


def rope_tables(positions, head_dim):
    half_dim = head_dim // 2
    frequency = jnp.exp(
        jnp.arange(half_dim, dtype=jnp.float32) * (-2.0 * math.log(rope_base) / head_dim)
    )
    angles = positions.astype(jnp.float32)[:, None] * frequency[None, :]
    return (jnp.cos(angles)[:, None, :], jnp.sin(angles)[:, None, :])


def rotate(tensor, cos_table, sin_table):
    half_dim = tensor.shape[-1] // 2
    first_half = tensor[..., :half_dim]
    second_half = tensor[..., half_dim:]
    return jnp.concatenate(
        [
            first_half * cos_table - second_half * sin_table,
            second_half * cos_table + first_half * sin_table,
        ],
        axis=-1,
    )


def rotate_back(tensor, cos_table, sin_table):
    half_dim = tensor.shape[-1] // 2
    first_half = tensor[..., :half_dim]
    second_half = tensor[..., half_dim:]
    return jnp.concatenate(
        [
            first_half * cos_table + second_half * sin_table,
            second_half * cos_table - first_half * sin_table,
        ],
        axis=-1,
    )


def rms_scale(hidden):
    factor = lax.rsqrt(jnp.mean(hidden * hidden, axis=-1, keepdims=True) + norm_eps)
    return (hidden * factor, factor)


def rms_back(grad_in, normed, factor, gain_row):
    scaled = grad_in * gain_row.astype(jnp.float32)
    return factor * (scaled - normed * jnp.mean(scaled * normed, axis=-1, keepdims=True))


def transposed_product(left, right):
    return jnp.einsum("tk,tn->kn", left, right, preferred_element_type=jnp.float32)


def gather_forward(params, layer_index):
    return (
        lax.all_gather(params[0][layer_index], "shard", axis=0, tiled=True),
        lax.all_gather(params[1][layer_index], "shard", axis=0, tiled=True),
        lax.all_gather(params[2][layer_index], "shard", axis=0, tiled=True),
        lax.all_gather(params[3][layer_index], "shard", axis=0, tiled=True),
        lax.all_gather(params[4][layer_index], "shard", axis=0, tiled=True),
        lax.all_gather(params[5][layer_index], "shard", axis=0, tiled=True),
        lax.all_gather(params[6][layer_index], "shard", axis=0, tiled=True),
        lax.all_gather(params[7][layer_index], "shard", axis=0, tiled=True),
        lax.all_gather(params[8][layer_index], "shard", axis=0, tiled=True),
    )


def gather_backward(params, layer_index):
    return (
        lax.all_gather(params[0][layer_index], "shard", axis=0, tiled=True),
        lax.all_gather(params[1][layer_index], "shard", axis=0, tiled=True),
        lax.all_gather(params[2][layer_index], "shard", axis=0, tiled=True),
        lax.all_gather(params[3][layer_index], "shard", axis=0, tiled=True),
        lax.all_gather(params[4][layer_index], "shard", axis=0, tiled=True),
        lax.all_gather(params[5][layer_index], "shard", axis=0, tiled=True),
        lax.all_gather(params[6][layer_index], "shard", axis=0, tiled=True),
        lax.all_gather(params[7][layer_index], "shard", axis=0, tiled=True),
        lax.all_gather(params[8][layer_index], "shard", axis=0, tiled=True),
    )


def visible_scores(query_grouped, all_keys, q_positions, key_positions):
    scores = jnp.einsum(
        "sgmd,tgd->gmst", query_grouped, all_keys, preferred_element_type=jnp.float32
    ) * HD ** (-0.5)
    allowed = key_positions[None, :] <= q_positions[:, None]
    return (jnp.where(allowed, scores, -1e30), allowed)


def layer_forward(hidden, gathered, q_positions, key_positions, cos_table, sin_table):
    attn_g, q_w, k_w, v_w, o_w, ffn_g, gate_w, up_w, down_w = gathered
    row_count = hidden.shape[0]
    head_groups = H // KV
    normed, factor = rms_scale(hidden)
    attn_in = (normed * attn_g.astype(jnp.float32)).astype(jnp.bfloat16)
    query_rows = rotate(
        jnp.dot(attn_in, q_w, preferred_element_type=jnp.float32).reshape(row_count, H, HD),
        cos_table,
        sin_table,
    ).astype(jnp.bfloat16)
    key_rows = rotate(
        jnp.dot(attn_in, k_w, preferred_element_type=jnp.float32).reshape(row_count, KV, HD),
        cos_table,
        sin_table,
    ).astype(jnp.bfloat16)
    value_rows = jnp.dot(attn_in, v_w, preferred_element_type=jnp.float32).astype(jnp.bfloat16)
    all_keys, all_values = (
        lax.all_gather(key_rows.reshape(row_count, KV * HD), "shard", axis=0, tiled=True),
        lax.all_gather(value_rows, "shard", axis=0, tiled=True),
    )
    all_keys = all_keys.reshape(-1, KV, HD)
    all_values = all_values.reshape(-1, KV, HD)
    query_grouped = query_rows.reshape(row_count, KV, head_groups, HD)
    scores, allowed = visible_scores(query_grouped, all_keys, q_positions, key_positions)
    row_max = jnp.max(scores, axis=-1, keepdims=True)
    row_total = jnp.sum(jnp.exp(scores - row_max), axis=-1, keepdims=True)
    log_total = (row_max + jnp.log(row_total))[..., 0]
    probs_bf = jnp.where(allowed, jnp.exp(scores - log_total[..., None]), 0.0).astype(jnp.bfloat16)
    attended = (
        jnp.einsum("gmst,tgd->sgmd", probs_bf, all_values, preferred_element_type=jnp.float32)
        .astype(jnp.bfloat16)
        .reshape(row_count, H * HD)
    )
    middle = hidden + jnp.dot(attended, o_w, preferred_element_type=jnp.float32)
    normed_two, factor_two = rms_scale(middle)
    ffn_in = (normed_two * ffn_g.astype(jnp.float32)).astype(jnp.bfloat16)
    gate_pre = jnp.dot(ffn_in, gate_w, preferred_element_type=jnp.float32)
    up_pre = jnp.dot(ffn_in, up_w, preferred_element_type=jnp.float32)
    mixed = (jax.nn.silu(gate_pre) * up_pre).astype(jnp.bfloat16)
    output = middle + jnp.dot(mixed, down_w, preferred_element_type=jnp.float32)
    saved = (
        normed,
        factor,
        attn_in,
        query_grouped,
        all_keys,
        all_values,
        log_total,
        attended,
        normed_two,
        factor_two,
        ffn_in,
        gate_pre,
        up_pre,
        mixed,
    )
    return (output, saved)


def layer_backward(gradient, saved, gathered, q_positions, key_positions, cos_table, sin_table):
    attn_g, q_w, k_w, v_w, o_w, ffn_g, gate_w, up_w, down_w = gathered
    (
        normed,
        factor,
        attn_in,
        query_grouped,
        all_keys,
        all_values,
        log_total,
        attended,
        normed_two,
        factor_two,
        ffn_in,
        gate_pre,
        up_pre,
        mixed,
    ) = saved
    row_count = gradient.shape[0]
    head_groups = H // KV
    grad_bf = gradient.astype(jnp.bfloat16)
    g_down = transposed_product(mixed, grad_bf)
    g_mixed = jnp.einsum("tn,kn->tk", grad_bf, down_w, preferred_element_type=jnp.float32)
    sigmoid_gate = jax.nn.sigmoid(gate_pre)
    g_up = (g_mixed * gate_pre * sigmoid_gate).astype(jnp.bfloat16)
    g_gate = (g_mixed * up_pre * sigmoid_gate * (1.0 + gate_pre * (1.0 - sigmoid_gate))).astype(
        jnp.bfloat16
    )
    g_gate_w = transposed_product(ffn_in, g_gate)
    g_up_w = transposed_product(ffn_in, g_up)
    g_ffn_in = jnp.einsum(
        "tn,kn->tk", g_gate, gate_w, preferred_element_type=jnp.float32
    ) + jnp.einsum("tn,kn->tk", g_up, up_w, preferred_element_type=jnp.float32)
    g_ffn_gain = jnp.sum(g_ffn_in * normed_two, axis=0)
    g_middle = gradient + rms_back(g_ffn_in, normed_two, factor_two, ffn_g)
    middle_bf = g_middle.astype(jnp.bfloat16)
    g_o_w = transposed_product(attended, middle_bf)
    g_attended = (
        jnp.einsum("tn,kn->tk", middle_bf, o_w, preferred_element_type=jnp.float32)
        .astype(jnp.bfloat16)
        .reshape(row_count, KV, head_groups, HD)
    )
    scores, allowed = visible_scores(query_grouped, all_keys, q_positions, key_positions)
    probs = jnp.where(allowed, jnp.exp(scores - log_total[..., None]), 0.0)
    probs_bf = probs.astype(jnp.bfloat16)
    value_terms = jnp.einsum(
        "gmst,sgmd->tgd", probs_bf, g_attended, preferred_element_type=jnp.float32
    )
    g_probs = jnp.einsum(
        "sgmd,tgd->gmst", g_attended, all_values, preferred_element_type=jnp.float32
    )
    delta = jnp.einsum(
        "sgmd,sgmd->gms",
        g_attended,
        attended.reshape(row_count, KV, head_groups, HD),
        preferred_element_type=jnp.float32,
    )
    g_scores = (probs * (g_probs - delta[..., None]) * HD ** (-0.5)).astype(jnp.bfloat16)
    g_query = jnp.einsum("gmst,tgd->sgmd", g_scores, all_keys, preferred_element_type=jnp.float32)
    key_terms = jnp.einsum(
        "gmst,sgmd->tgd", g_scores, query_grouped, preferred_element_type=jnp.float32
    )
    seq_rows = key_terms.shape[0]
    key_sum, value_sum = (
        lax.psum_scatter(
            key_terms.reshape(seq_rows, KV * HD), "shard", scatter_dimension=0, tiled=True
        ),
        lax.psum_scatter(
            value_terms.reshape(seq_rows, KV * HD), "shard", scatter_dimension=0, tiled=True
        ),
    )
    g_query_bf = (
        rotate_back(g_query.reshape(row_count, H, HD), cos_table, sin_table)
        .reshape(row_count, H * HD)
        .astype(jnp.bfloat16)
    )
    g_key_bf = (
        rotate_back(key_sum.reshape(row_count, KV, HD), cos_table, sin_table)
        .reshape(row_count, KV * HD)
        .astype(jnp.bfloat16)
    )
    g_value_bf = value_sum.astype(jnp.bfloat16)
    g_q_w = transposed_product(attn_in, g_query_bf)
    g_k_w = transposed_product(attn_in, g_key_bf)
    g_v_w = transposed_product(attn_in, g_value_bf)
    g_attn_in = (
        jnp.einsum("tn,kn->tk", g_query_bf, q_w, preferred_element_type=jnp.float32)
        + jnp.einsum("tn,kn->tk", g_key_bf, k_w, preferred_element_type=jnp.float32)
        + jnp.einsum("tn,kn->tk", g_value_bf, v_w, preferred_element_type=jnp.float32)
    )
    g_attn_gain = jnp.sum(g_attn_in * normed, axis=0)
    g_hidden = g_middle + rms_back(g_attn_in, normed, factor, attn_g)
    terms = (g_attn_gain, g_q_w, g_k_w, g_v_w, g_o_w, g_ffn_gain, g_gate_w, g_up_w, g_down)
    return (g_hidden, terms)


def share_terms(terms):
    return (
        lax.psum_scatter(terms[0], "shard", scatter_dimension=0, tiled=True),
        lax.psum_scatter(terms[1], "shard", scatter_dimension=0, tiled=True),
        lax.psum_scatter(terms[2], "shard", scatter_dimension=0, tiled=True),
        lax.psum_scatter(terms[3], "shard", scatter_dimension=0, tiled=True),
        lax.psum_scatter(terms[4], "shard", scatter_dimension=0, tiled=True),
        lax.psum_scatter(terms[5], "shard", scatter_dimension=0, tiled=True),
        lax.psum_scatter(terms[6], "shard", scatter_dimension=0, tiled=True),
        lax.psum_scatter(terms[7], "shard", scatter_dimension=0, tiled=True),
        lax.psum_scatter(terms[8], "shard", scatter_dimension=0, tiled=True),
    )


def replica_sum(shares):
    return lax.psum(
        (
            shares[0],
            shares[1],
            shares[2],
            shares[3],
            shares[4],
            shares[5],
            shares[6],
            shares[7],
            shares[8],
        ),
        "rep",
    )


def body(
    tokens,
    block_order,
    attn_gain,
    q_weight,
    k_weight,
    v_weight,
    o_weight,
    ffn_gain,
    gate_weight,
    up_weight,
    down_weight,
    cotangent,
):
    row_count = tokens.shape[0]
    order_row = block_order[0]
    own_block = lax.dynamic_index_in_dim(order_row, lax.axis_index("shard"), 0, keepdims=False)
    local_index = jnp.arange(row_count, dtype=jnp.int32)
    q_positions = own_block * row_count + local_index
    key_positions = (order_row[:, None] * row_count + local_index[None, :]).reshape(-1)
    cos_table, sin_table = rope_tables(q_positions, HD)
    params = (
        attn_gain,
        q_weight,
        k_weight,
        v_weight,
        o_weight,
        ffn_gain,
        gate_weight,
        up_weight,
        down_weight,
    )
    hidden = tokens.astype(jnp.float32)
    kept_weights = []
    layer_index = 0
    gathered = gather_forward(params, layer_index)
    hidden, saved = layer_forward(
        hidden, gathered, q_positions, key_positions, cos_table, sin_table
    )
    saved_list = [saved]
    kept_weights.append(gathered)
    gradient = cotangent.astype(jnp.float32)
    reduced = [None] * LAYERS
    for layer_index in reversed(range(LAYERS)):
        gathered = gather_backward(params, layer_index)
        gradient, terms = layer_backward(
            gradient,
            saved_list[layer_index],
            gathered,
            q_positions,
            key_positions,
            cos_table,
            sin_table,
        )
        shares = replica_sum(share_terms(terms))
        reduced[layer_index] = shares
    stacked = tuple((jnp.stack([reduced[0][member]]) for member in range(9)))
    return (
        hidden,
        gradient,
        stacked[0],
        stacked[1],
        stacked[2],
        stacked[3],
        stacked[4],
        stacked[5],
        stacked[6],
        stacked[7],
        stacked[8],
    )


F32 = jnp.float32
BF16 = jnp.bfloat16
MESH = pl.DeviceIdType.MESH


def nn(left, right):
    return lax.dot_general(left, right, (((1,), (0,)), ((), ())), preferred_element_type=F32)


def nt(left, right):
    return lax.dot_general(left, right, (((1,), (1,)), ((), ())), preferred_element_type=F32)


def tn(left, right):
    return lax.dot_general(left, right, (((0,), (0,)), ((), ())), preferred_element_type=F32)


def swap_halves(x):
    width = x.shape[-1]
    lane = lax.broadcasted_iota(jnp.int32, x.shape, 1)
    return jnp.where(
        lane % HD < HD // 2, pltpu.roll(x, width - HD // 2, 1), pltpu.roll(x, HD // 2, 1)
    )


def fused_kernel(
    tok_ref, cot_ref, cos_ref, sin_ref, bias_ref, gain_ref, wa_ref, gate_ref, up_ref, down_ref,
    out_ref, gin_ref, o1_ref, o2_ref, o3_ref,
    wa, wg, wu, gain_in, cot, kv, bb, part_out, part_in, dbo, dbi, probs, a_half, t_half, dm_x,
    dkv_out, dkv_in, dqk_x, dv_x, gg_out, gg_in, g1, g2, g3, r1a, r1b, r1c, r2a, r2b, r2c,
    r3a, r3b, r3c, f1, f2, f3, send_sem, recv_sem, local_sem,
):
    rows = tok_ref.shape[0]
    rep = lax.axis_index("rep")
    s = lax.axis_index("shard")
    core = rep % 2
    y = (rep // 2) % 2
    z = rep // 4
    xpeer = (rep, 1 - s)
    cpeer = (rep + 1 - 2 * core, s)
    ypeer = (rep + 2 - 4 * y, s)

    def zdev(z2):
        return (z2 * 4 + y * 2 + core, s)

    zpeers = [zdev((z + d) % 4) for d in (1, 2, 3)]
    counter = [0]
    started = []

    def remote(src, dst, device):
        i = counter[0]
        counter[0] += 1
        c = pltpu.make_async_remote_copy(
            src_ref=src, dst_ref=dst, send_sem=send_sem.at[i], recv_sem=recv_sem.at[i],
            device_id=device, device_id_type=MESH,
        )
        c.start()
        started.append(c)
        return c

    half = wa_ref.shape[0]
    ffh = wg.shape[1]
    mine = pl.multiple_of(s * half, 16)
    theirs = pl.multiple_of((1 - s) * half, 16)
    local = [
        pltpu.make_async_copy(wa_ref, wa.at[pl.ds(mine, half), :], local_sem.at[0]),
        pltpu.make_async_copy(
            gate_ref.at[:, pl.ds(pl.multiple_of(s * ffh, 128), ffh)],
            wg.at[pl.ds(mine, half), :], local_sem.at[1],
        ),
        pltpu.make_async_copy(
            up_ref.at[:, pl.ds(pl.multiple_of(s * ffh, 128), ffh)],
            wu.at[pl.ds(mine, half), :], local_sem.at[2],
        ),
    ]
    for c in local:
        c.start()

    barrier = pltpu.get_barrier_semaphore()
    for peer in [xpeer, cpeer, ypeer] + zpeers:
        pl.semaphore_signal(barrier, inc=1, device_id=peer, device_id_type=MESH)
    pl.semaphore_wait(barrier, 6)

    gain_copy = remote(gain_ref, gain_in, xpeer)
    hr = half // 2
    targets = [(wa_ref, wa, 0), (gate_ref, wg, ffh), (up_ref, wu, ffh)]
    xcopies = []
    for src, dst, other in targets:
        hc = dst.shape[1] // 2
        xcopies.append(
            remote(
                src.at[
                    pl.ds(pl.multiple_of(y * hr, 16), hr),
                    pl.ds(pl.multiple_of((1 - s) * other + core * hc, 128), hc),
                ],
                dst.at[
                    pl.ds(pl.multiple_of(s * half + y * hr, 16), hr),
                    pl.ds(pl.multiple_of(core * hc, 128), hc),
                ],
                xpeer,
            )
        )
    cot_copy = remote(cot_ref, cot, xpeer)

    def ystep(i):
        dst = targets[i][1]
        hc = dst.shape[1] // 2
        xcopies[i].wait_recv()
        block = dst.at[
            pl.ds(pl.multiple_of((1 - s) * half + y * hr, 16), hr),
            pl.ds(pl.multiple_of(core * hc, 128), hc),
        ]
        return remote(block, block, ypeer)

    def cstep(i, ycopy):
        dst = targets[i][1]
        hc = dst.shape[1] // 2
        ycopy.wait_recv()
        block = dst.at[
            pl.ds(theirs, half), pl.ds(pl.multiple_of(core * hc, 128), hc)
        ]
        return remote(block, block, cpeer)

    ya = ystep(0)
    hidden = tok_ref[...].astype(F32)
    rr = lax.rsqrt(jnp.mean(hidden * hidden, axis=-1, keepdims=True) + norm_eps)
    normed = hidden * rr
    gain_copy.wait_recv()
    gains = gain_ref[...].astype(F32) + gain_in[...].astype(F32)
    attn_g = gains[0:1, :]
    ffn_g = gains[1:2, :]
    attn_in = (normed * attn_g).astype(BF16)
    yg = ystep(1)
    ca = cstep(0, ya)
    yu = ystep(2)
    dm = attn_in.shape[1] // 2

    def pick(value, flag):
        return jnp.where(flag == 0, value[:, :dm], value[:, dm:])

    for c in local:
        c.wait()
    ca.wait_recv()
    qk = nn(attn_in, wa[:, :768])
    cos_t = cos_ref[...]
    sin_t = sin_ref[...]
    qk = (qk * cos_t + swap_halves(qk) * sin_t).astype(BF16)
    v = nn(attn_in, wa[:, 1280:1536])[:, 64:256].astype(BF16)
    kv_own = jnp.concatenate([qk[:, 576:768], v], axis=1)
    kv[0] = kv_own
    kv_copy = remote(kv.at[0], kv.at[1], xpeer)
    a_half[0] = pick(attn_in, s)
    a_half[1] = pick(attn_in, 1 - s)
    cg = cstep(1, yg)
    cu = cstep(2, yu)
    kv_copy.wait_recv()
    kv_oth = kv[1]
    groups = H // KV
    bias = bias_ref[...]
    bias3 = jnp.concatenate([bias] * groups, axis=0)

    def stack(value, g):
        return jnp.concatenate(
            [value[:, HD * j : HD * (j + 1)] for j in range(g * groups, (g + 1) * groups)], axis=0
        )

    def unstack(values):
        return [v[i * rows : (i + 1) * rows] for v in values for i in range(groups)]

    def keys(off, g):
        lo = off + HD * g
        return jnp.concatenate([kv_own[:, lo : lo + HD], kv_oth[:, lo : lo + HD]], axis=0)

    qs = [stack(qk, g) for g in range(KV)]
    ks = [keys(0, g) for g in range(KV)]
    vs = [keys(KV * HD, g) for g in range(KV)]
    outs = []
    for g in range(KV):
        sc = nt(qs[g], ks[g]) * HD ** (-0.5) + bias3
        top = jnp.max(sc, axis=-1, keepdims=True)
        lse = top + jnp.log(jnp.sum(jnp.exp(sc - top), axis=-1, keepdims=True))
        p = jnp.exp(sc - lse)
        probs[g] = p
        outs.append(nn(p.astype(BF16), vs[g]).astype(BF16))
    attended = jnp.concatenate(unstack(outs), axis=1)
    w_o = wa[:, 768:1344]
    middle = hidden + nn(attended, w_o)
    rr2 = lax.rsqrt(jnp.mean(middle * middle, axis=-1, keepdims=True) + norm_eps)
    normed2 = middle * rr2
    bb[0:rows] = (normed2 * ffn_g).astype(BF16)
    b_copy = remote(bb.at[pl.ds(0, rows)], bb.at[pl.ds(rows, rows)], xpeer)
    t_half[0] = pick(attended, s)
    t_half[1] = pick(attended, 1 - s)
    a_copy = remote(a_half.at[1], a_half.at[2], xpeer)
    cot_copy.wait_recv()
    grad_all = jnp.concatenate([cot_ref[...], cot[...]], axis=0)
    d_mix = nt(grad_all, down_ref[...])
    cg.wait_recv()
    cu.wait_recv()
    b_copy.wait_recv()
    ball = bb[...]
    gt = nn(ball, wg[...])
    up = nn(ball, wu[...])
    sig = jax.nn.sigmoid(gt)
    silu = gt * sig
    mix = (silu * up).astype(BF16)
    d_up = (d_mix * silu).astype(BF16)
    d_gt = (d_mix * up * sig * (1.0 + gt * (1.0 - sig))).astype(BF16)
    db = nt(d_gt, wg[...]) + nt(d_up, wu[...])
    dbo[...] = db[rows:].astype(BF16)
    db_copy = remote(dbo, dbi, xpeer)
    part = nn(mix, down_ref[...])
    part_out[...] = part[rows:].astype(BF16)
    part_copy = remote(part_out, part_in, xpeer)
    t_copy = remote(t_half.at[1], t_half.at[2], xpeer)

    gs, r1, r2, r3 = (g2, g1, g3), (r1b, r1a, r1c), (r2b, r2a, r2c), (r3b, r3a, r3c)
    fs, res = (f2, f1, f3), (o2_ref, o1_ref, o3_ref)
    state = [None] * 3

    def rs_core(p):
        state[p] = remote(gs[p].at[pl.ds((1 - core) * 8, 8)], r1[p], cpeer)

    def rs_y(p):
        state[p].wait_recv()

        @pl.loop(0, 8)
        def _(k):
            r1[p][k] = (r1[p][k].astype(F32) + gs[p][core * 8 + k].astype(F32)).astype(BF16)

        state[p] = remote(r1[p].at[pl.ds((1 - y) * 4, 4)], r2[p], ypeer)

    def rs_z(p):
        state[p].wait_recv()

        @pl.loop(0, 4)
        def _(k):
            r2[p][k] = (r2[p][k].astype(F32) + r1[p][y * 4 + k].astype(F32)).astype(BF16)

        state[p] = [
            remote(r2[p].at[(z + d) % 4], r3[p].at[d - 1], zpeers[d - 1]) for d in (1, 2, 3)
        ]

    def ag_z(p):
        for c in state[p]:
            c.wait_recv()
        total = r2[p][z].astype(F32)
        for d in range(3):
            total = total + r3[p][d].astype(F32)
        slot = core
        if p == 1:
            fs[p][0] = total.astype(BF16)
            i = counter[0]
            counter[0] += 1
            swap = pltpu.make_async_remote_copy(
                src_ref=fs[p].at[0], dst_ref=fs[p].at[1], send_sem=send_sem.at[i],
                recv_sem=recv_sem.at[i], device_id=xpeer, device_id_type=MESH,
            )

            @pl.when(core == 1)
            def _():
                swap.start()
                swap.wait()
                fs[p][0] = fs[p][1]

            slot = jnp.where(s == 0, core, 1 - core)
            res[p][slot * 8 + y * 4 + z] = fs[p][0]
        else:
            fs[p][0] = total.astype(BF16)
            res[p][slot * 8 + y * 4 + z] = fs[p][0]
        place = slot * 8 + y * 4 + z
        state[p] = [
            remote(fs[p].at[0], res[p].at[place], zpeers[d - 1]) for d in (1, 2, 3)
        ]
        return slot

    slots = [None] * 3

    def ag_y(p):
        for c in state[p]:
            c.wait_recv()
        block = res[p].at[pl.ds(slots[p] * 8 + y * 4, 4)]
        state[p] = remote(block, block, ypeer)

    def ag_core(p):
        state[p].wait_recv()
        block = res[p].at[pl.ds(slots[p] * 8, 8)]
        state[p] = remote(block, block, cpeer)

    g2[...] = tn(mix, grad_all).astype(BF16).reshape(g2.shape)
    rs_core(0)
    for half_t, dd in enumerate((d_gt, d_up)):
        gw = tn(ball, dd).astype(BF16)
        for h in range(2):
            for yy in range(2):
                for zz in range(2):
                    k = jnp.where(s == h, 0, 8) + yy * 4 + half_t * 2 + zz
                    lo = h * half + yy * hr
                    g1[k] = gw[lo : lo + hr, zz * 384 : (zz + 1) * 384]
    rs_core(1)
    db_copy.wait_recv()
    db = db[:rows] + dbi[...].astype(F32)
    gain2 = jnp.sum(db * normed2, axis=0, keepdims=True)
    e = db * ffn_g
    dm1 = cot_ref[...].astype(F32) + rr2 * (
        e - normed2 * jnp.mean(e * normed2, axis=-1, keepdims=True)
    )
    dm1b = dm1.astype(BF16)
    dm_x[0] = dm1b
    dm_copy = remote(dm_x.at[0], dm_x.at[1], xpeer)
    d_att = nt(dm1b, w_o).astype(BF16)
    rs_y(0)
    part_copy.wait_recv()
    out_ref[...] = middle + part[:rows] + part_in[...].astype(F32)

    dqs, dks, dvs = [], [], []
    for g in range(KV):
        do_g = stack(d_att, g)
        p = probs[g]
        dvs.append(tn(p.astype(BF16), do_g))
        delta = jnp.sum(do_g.astype(F32) * outs[g].astype(F32), axis=-1, keepdims=True)
        ds = (p * (nt(do_g, vs[g]) - delta) * HD ** (-0.5)).astype(BF16)
        dqs.append(nn(ds, ks[g]))
        dks.append(tn(ds, qs[g]))
        if g == 0:
            rs_y(1)
    dkv = jnp.concatenate(dks + dvs, axis=1)
    dkv_out[...] = dkv[rows:].astype(BF16)
    dkv_copy = remote(dkv_out, dkv_in, xpeer)
    rs_z(0)
    dkv_copy.wait_recv()
    dkv = dkv[:rows] + dkv_in[...].astype(F32)
    dqk = jnp.concatenate(unstack(dqs) + [dkv[:, : KV * HD]], axis=1)
    dqk = (dqk * cos_t - swap_halves(dqk) * sin_t).astype(BF16)
    dvb = dkv[:, KV * HD :].astype(BF16)
    dqk_x[0] = dqk
    dv_x[0] = dvb
    dqk_copy = remote(dqk_x.at[0], dqk_x.at[1], xpeer)
    dv_copy = remote(dv_x.at[0], dv_x.at[1], xpeer)
    da = nt(dqk, wa[:, :768]) + nt(
        jnp.concatenate([jnp.zeros((rows, 64), BF16), dvb], axis=1), wa[:, 1280:1536]
    )
    gain1 = jnp.sum(da * normed, axis=0, keepdims=True)
    gg_out[...] = jnp.concatenate([gain1, gain2, jnp.zeros((6, gain1.shape[1]), F32)], axis=0)
    gg_copy = remote(gg_out, gg_in, xpeer)
    rs_z(1)
    f = da * attn_g
    gin_ref[...] = dm1 + rr * (f - normed * jnp.mean(f * normed, axis=-1, keepdims=True))
    for c in (a_copy, t_copy, dm_copy, dqk_copy, dv_copy):
        c.wait_recv()
    a_all = jnp.concatenate([a_half[0], a_half[2]], axis=0)
    t_all = jnp.concatenate([t_half[0], t_half[2]], axis=0)
    gw_o = tn(t_all, jnp.concatenate([dm_x[0], dm_x[1]], axis=0)).astype(BF16)
    gw_qk = tn(a_all, jnp.concatenate([dqk_x[0], dqk_x[1]], axis=0)).astype(BF16)
    gw_v = tn(a_all, jnp.concatenate([dv_x[0], dv_x[1]], axis=0)).astype(BF16)
    columns = [
        gw_qk[:, :384], gw_qk[:, 384:], gw_o[:, :384],
        jnp.concatenate([gw_o[:, 384:], gw_v], axis=1),
    ]
    gg_copy.wait_recv()
    gg = pick(gg_out[...] + gg_in[...], s)
    gg = jnp.concatenate([gg, jnp.zeros((8, 384 - dm), F32)], axis=1)
    row32 = lax.broadcasted_iota(jnp.int32, (32, 384), 0)
    for cc in range(4):
        for r in range(3):
            g3[r * 4 + cc] = columns[cc][r * 80 : (r + 1) * 80]
        g3[12 + cc, 0:48] = columns[cc][240:288]
        if cc < 2:
            tail = jnp.where(row32 == 0, jnp.broadcast_to(gg[cc : cc + 1], (32, 384)), 0.0)
        else:
            tail = jnp.zeros((32, 384), F32)
        g3[12 + cc, 48:80] = tail.astype(BF16)
    rs_core(2)
    slots[0] = ag_z(0)
    rs_y(2)
    slots[1] = ag_z(1)
    rs_z(2)
    ag_y(0)
    slots[2] = ag_z(2)
    ag_y(1)
    ag_core(0)
    ag_y(2)
    ag_core(1)
    ag_core(2)
    for st in state:
        st.wait_recv()
    for c in started:
        c.wait_send()


def fused_body(
    tokens, block_order, attn_gain, q_weight, k_weight, v_weight, o_weight, ffn_gain,
    gate_weight, up_weight, down_weight, cotangent,
):
    rows, width = tokens.shape
    s = lax.axis_index("shard")
    half = attn_gain.shape[1]
    ff = gate_weight.shape[2]
    order = block_order[0]
    own = lax.dynamic_index_in_dim(order, s, 0, keepdims=False)
    other = lax.dynamic_index_in_dim(order, 1 - s, 0, keepdims=False)
    index = jnp.arange(rows, dtype=jnp.int32)
    q_pos = own * rows + index
    k_pos = jnp.concatenate([q_pos, other * rows + index])
    bias = jnp.where(k_pos[None, :] <= q_pos[:, None], 0.0, -1e30).astype(F32)
    cos_t, sin_t = rope_tables(q_pos, HD)
    cos_t, sin_t = cos_t[:, 0], sin_t[:, 0]
    cos_t = jnp.tile(cos_t, (1, 2 * (H + KV)))
    sin_t = jnp.tile(jnp.concatenate([-sin_t, sin_t], axis=1), (1, H + KV))
    gains = jnp.concatenate([attn_gain, ffn_gain, jnp.zeros((14, half), BF16)], axis=0)
    gains = jnp.concatenate(
        [jnp.where(s == 0, gains, 0), jnp.where(s == 1, gains, 0)], axis=1
    ).astype(BF16)
    wa = jnp.concatenate([q_weight[0], k_weight[0], o_weight[0], v_weight[0]], axis=1)
    vm = pl.BlockSpec(memory_space=pltpu.VMEM)
    shapes = [(144, 384), (48, width), (80, 384)]

    def buf(*shape, dtype=BF16):
        return pltpu.VMEM(shape, dtype)

    scratch = [
        buf(width, 1536), buf(width, ff // 2), buf(width, ff // 2), buf(16, width),
        buf(rows, width), buf(2, rows, 384), buf(2 * rows, width), buf(rows, width),
        buf(rows, width), buf(rows, width), buf(rows, width),
        buf(KV, 3 * rows, 2 * rows, dtype=F32), buf(3, rows, half), buf(3, rows, half),
        buf(2, rows, width), buf(rows, 384), buf(rows, 384), buf(2, rows, 768),
        buf(2, rows, 192), buf(8, width, dtype=F32), buf(8, width, dtype=F32),
    ]
    for count in (16, 8, 4, 3, 2):
        scratch += [buf(count, *sh) for sh in shapes]
    scratch += [
        pltpu.SemaphoreType.DMA((64,)), pltpu.SemaphoreType.DMA((64,)),
        pltpu.SemaphoreType.DMA((3,)),
    ]
    block_out, input_grad, o1, o2, o3 = pl.pallas_call(
        fused_kernel,
        out_shape=(
            jax.ShapeDtypeStruct((rows, width), F32),
            jax.ShapeDtypeStruct((rows, width), F32),
            *[jax.ShapeDtypeStruct((16, *sh), BF16) for sh in shapes],
        ),
        in_specs=[vm] * 10,
        out_specs=[vm] * 5,
        scratch_shapes=scratch,
        compiler_params=pltpu.CompilerParams(
            collective_id=0, has_side_effects=True, vmem_limit_bytes=56 * 1024 * 1024
        ),
    )(
        tokens, cotangent, cos_t, sin_t, bias, gains, wa, gate_weight[0], up_weight[0],
        down_weight[0],
    )
    gu = o1.reshape(2, 2, 2, 2, 144, 384)
    gu = gu.transpose(2, 1, 4, 0, 3, 5).reshape(2, half, ff).astype(F32)
    rest = o3.reshape(4, 4, 80, 384).transpose(0, 2, 1, 3).reshape(320, 1536).astype(F32)
    return (
        block_out,
        input_grad,
        rest[288:289, :288],
        rest[None, :288, :576],
        rest[None, :288, 576:768],
        rest[None, :288, 1344:],
        rest[None, :288, 768:1344],
        rest[288:289, 384 : 384 + 288],
        gu[0:1],
        gu[1:2],
        o2.reshape(1, 768, width).astype(F32),
    )


def solution(mesh):
    placed = (
        P(("rep", "shard"), None),
        P("rep", None),
        P(None, "shard"),
        P(None, "shard", None),
        P(None, "shard", None),
        P(None, "shard", None),
        P(None, "shard", None),
        P(None, "shard"),
        P(None, "shard", None),
        P(None, "shard", None),
        P(None, "shard", None),
        P(("rep", "shard"), None),
    )
    fused = mesh.shape["shard"] == 2 and mesh.shape["rep"] == 16
    return jax.shard_map(
        fused_body if fused else body,
        mesh=mesh,
        in_specs=placed,
        out_specs=(
            P(("rep", "shard"), None),
            P(("rep", "shard"), None),
            P(None, "shard"),
            P(None, "shard", None),
            P(None, "shard", None),
            P(None, "shard", None),
            P(None, "shard", None),
            P(None, "shard"),
            P(None, "shard", None),
            P(None, "shard", None),
            P(None, "shard", None),
        ),
        check_vma=False,
    )
```

```python
import math

import jax
import jax.numpy as jnp
from jax import lax
from jax.experimental import pallas as pl
from jax.experimental.pallas import tpu as pltpu
from jax.sharding import PartitionSpec as P

H = 9
KV = 3
HD = 64
LAYERS = 1


rope_base = 100000.0
norm_eps = 1e-05


def rope_tables(positions, head_dim):
    half_dim = head_dim // 2
    frequency = jnp.exp(
        jnp.arange(half_dim, dtype=jnp.float32) * (-2.0 * math.log(rope_base) / head_dim)
    )
    angles = positions.astype(jnp.float32)[:, None] * frequency[None, :]
    return (jnp.cos(angles)[:, None, :], jnp.sin(angles)[:, None, :])


def rotate(tensor, cos_table, sin_table):
    half_dim = tensor.shape[-1] // 2
    first_half = tensor[..., :half_dim]
    second_half = tensor[..., half_dim:]
    return jnp.concatenate(
        [
            first_half * cos_table - second_half * sin_table,
            second_half * cos_table + first_half * sin_table,
        ],
        axis=-1,
    )


def rotate_back(tensor, cos_table, sin_table):
    half_dim = tensor.shape[-1] // 2
    first_half = tensor[..., :half_dim]
    second_half = tensor[..., half_dim:]
    return jnp.concatenate(
        [
            first_half * cos_table + second_half * sin_table,
            second_half * cos_table - first_half * sin_table,
        ],
        axis=-1,
    )


def rms_scale(hidden):
    factor = lax.rsqrt(jnp.mean(hidden * hidden, axis=-1, keepdims=True) + norm_eps)
    return (hidden * factor, factor)


def rms_back(grad_in, normed, factor, gain_row):
    scaled = grad_in * gain_row.astype(jnp.float32)
    return factor * (scaled - normed * jnp.mean(scaled * normed, axis=-1, keepdims=True))


def transposed_product(left, right):
    return jnp.einsum("tk,tn->kn", left, right, preferred_element_type=jnp.float32)


def gather_forward(params, layer_index):
    return (
        lax.all_gather(params[0][layer_index], "shard", axis=0, tiled=True),
        lax.all_gather(params[1][layer_index], "shard", axis=0, tiled=True),
        lax.all_gather(params[2][layer_index], "shard", axis=0, tiled=True),
        lax.all_gather(params[3][layer_index], "shard", axis=0, tiled=True),
        lax.all_gather(params[4][layer_index], "shard", axis=0, tiled=True),
        lax.all_gather(params[5][layer_index], "shard", axis=0, tiled=True),
        lax.all_gather(params[6][layer_index], "shard", axis=0, tiled=True),
        lax.all_gather(params[7][layer_index], "shard", axis=0, tiled=True),
        lax.all_gather(params[8][layer_index], "shard", axis=0, tiled=True),
    )


def gather_backward(params, layer_index):
    return (
        lax.all_gather(params[0][layer_index], "shard", axis=0, tiled=True),
        lax.all_gather(params[1][layer_index], "shard", axis=0, tiled=True),
        lax.all_gather(params[2][layer_index], "shard", axis=0, tiled=True),
        lax.all_gather(params[3][layer_index], "shard", axis=0, tiled=True),
        lax.all_gather(params[4][layer_index], "shard", axis=0, tiled=True),
        lax.all_gather(params[5][layer_index], "shard", axis=0, tiled=True),
        lax.all_gather(params[6][layer_index], "shard", axis=0, tiled=True),
        lax.all_gather(params[7][layer_index], "shard", axis=0, tiled=True),
        lax.all_gather(params[8][layer_index], "shard", axis=0, tiled=True),
    )


def visible_scores(query_grouped, all_keys, q_positions, key_positions):
    scores = jnp.einsum(
        "sgmd,tgd->gmst", query_grouped, all_keys, preferred_element_type=jnp.float32
    ) * HD ** (-0.5)
    allowed = key_positions[None, :] <= q_positions[:, None]
    return (jnp.where(allowed, scores, -1e30), allowed)


def layer_forward(hidden, gathered, q_positions, key_positions, cos_table, sin_table):
    attn_g, q_w, k_w, v_w, o_w, ffn_g, gate_w, up_w, down_w = gathered
    row_count = hidden.shape[0]
    head_groups = H // KV
    normed, factor = rms_scale(hidden)
    attn_in = (normed * attn_g.astype(jnp.float32)).astype(jnp.bfloat16)
    query_rows = rotate(
        jnp.dot(attn_in, q_w, preferred_element_type=jnp.float32).reshape(row_count, H, HD),
        cos_table,
        sin_table,
    ).astype(jnp.bfloat16)
    key_rows = rotate(
        jnp.dot(attn_in, k_w, preferred_element_type=jnp.float32).reshape(row_count, KV, HD),
        cos_table,
        sin_table,
    ).astype(jnp.bfloat16)
    value_rows = jnp.dot(attn_in, v_w, preferred_element_type=jnp.float32).astype(jnp.bfloat16)
    all_keys, all_values = (
        lax.all_gather(key_rows.reshape(row_count, KV * HD), "shard", axis=0, tiled=True),
        lax.all_gather(value_rows, "shard", axis=0, tiled=True),
    )
    all_keys = all_keys.reshape(-1, KV, HD)
    all_values = all_values.reshape(-1, KV, HD)
    query_grouped = query_rows.reshape(row_count, KV, head_groups, HD)
    scores, allowed = visible_scores(query_grouped, all_keys, q_positions, key_positions)
    row_max = jnp.max(scores, axis=-1, keepdims=True)
    row_total = jnp.sum(jnp.exp(scores - row_max), axis=-1, keepdims=True)
    log_total = (row_max + jnp.log(row_total))[..., 0]
    probs_bf = jnp.where(allowed, jnp.exp(scores - log_total[..., None]), 0.0).astype(jnp.bfloat16)
    attended = (
        jnp.einsum("gmst,tgd->sgmd", probs_bf, all_values, preferred_element_type=jnp.float32)
        .astype(jnp.bfloat16)
        .reshape(row_count, H * HD)
    )
    middle = hidden + jnp.dot(attended, o_w, preferred_element_type=jnp.float32)
    normed_two, factor_two = rms_scale(middle)
    ffn_in = (normed_two * ffn_g.astype(jnp.float32)).astype(jnp.bfloat16)
    gate_pre = jnp.dot(ffn_in, gate_w, preferred_element_type=jnp.float32)
    up_pre = jnp.dot(ffn_in, up_w, preferred_element_type=jnp.float32)
    mixed = (jax.nn.silu(gate_pre) * up_pre).astype(jnp.bfloat16)
    output = middle + jnp.dot(mixed, down_w, preferred_element_type=jnp.float32)
    saved = (
        normed,
        factor,
        attn_in,
        query_grouped,
        all_keys,
        all_values,
        log_total,
        attended,
        normed_two,
        factor_two,
        ffn_in,
        gate_pre,
        up_pre,
        mixed,
    )
    return (output, saved)


def layer_backward(gradient, saved, gathered, q_positions, key_positions, cos_table, sin_table):
    attn_g, q_w, k_w, v_w, o_w, ffn_g, gate_w, up_w, down_w = gathered
    (
        normed,
        factor,
        attn_in,
        query_grouped,
        all_keys,
        all_values,
        log_total,
        attended,
        normed_two,
        factor_two,
        ffn_in,
        gate_pre,
        up_pre,
        mixed,
    ) = saved
    row_count = gradient.shape[0]
    head_groups = H // KV
    grad_bf = gradient.astype(jnp.bfloat16)
    g_down = transposed_product(mixed, grad_bf)
    g_mixed = jnp.einsum("tn,kn->tk", grad_bf, down_w, preferred_element_type=jnp.float32)
    sigmoid_gate = jax.nn.sigmoid(gate_pre)
    g_up = (g_mixed * gate_pre * sigmoid_gate).astype(jnp.bfloat16)
    g_gate = (g_mixed * up_pre * sigmoid_gate * (1.0 + gate_pre * (1.0 - sigmoid_gate))).astype(
        jnp.bfloat16
    )
    g_gate_w = transposed_product(ffn_in, g_gate)
    g_up_w = transposed_product(ffn_in, g_up)
    g_ffn_in = jnp.einsum(
        "tn,kn->tk", g_gate, gate_w, preferred_element_type=jnp.float32
    ) + jnp.einsum("tn,kn->tk", g_up, up_w, preferred_element_type=jnp.float32)
    g_ffn_gain = jnp.sum(g_ffn_in * normed_two, axis=0)
    g_middle = gradient + rms_back(g_ffn_in, normed_two, factor_two, ffn_g)
    middle_bf = g_middle.astype(jnp.bfloat16)
    g_o_w = transposed_product(attended, middle_bf)
    g_attended = (
        jnp.einsum("tn,kn->tk", middle_bf, o_w, preferred_element_type=jnp.float32)
        .astype(jnp.bfloat16)
        .reshape(row_count, KV, head_groups, HD)
    )
    scores, allowed = visible_scores(query_grouped, all_keys, q_positions, key_positions)
    probs = jnp.where(allowed, jnp.exp(scores - log_total[..., None]), 0.0)
    probs_bf = probs.astype(jnp.bfloat16)
    value_terms = jnp.einsum(
        "gmst,sgmd->tgd", probs_bf, g_attended, preferred_element_type=jnp.float32
    )
    g_probs = jnp.einsum(
        "sgmd,tgd->gmst", g_attended, all_values, preferred_element_type=jnp.float32
    )
    delta = jnp.einsum(
        "sgmd,sgmd->gms",
        g_attended,
        attended.reshape(row_count, KV, head_groups, HD),
        preferred_element_type=jnp.float32,
    )
    g_scores = (probs * (g_probs - delta[..., None]) * HD ** (-0.5)).astype(jnp.bfloat16)
    g_query = jnp.einsum("gmst,tgd->sgmd", g_scores, all_keys, preferred_element_type=jnp.float32)
    key_terms = jnp.einsum(
        "gmst,sgmd->tgd", g_scores, query_grouped, preferred_element_type=jnp.float32
    )
    seq_rows = key_terms.shape[0]
    key_sum, value_sum = (
        lax.psum_scatter(
            key_terms.reshape(seq_rows, KV * HD), "shard", scatter_dimension=0, tiled=True
        ),
        lax.psum_scatter(
            value_terms.reshape(seq_rows, KV * HD), "shard", scatter_dimension=0, tiled=True
        ),
    )
    g_query_bf = (
        rotate_back(g_query.reshape(row_count, H, HD), cos_table, sin_table)
        .reshape(row_count, H * HD)
        .astype(jnp.bfloat16)
    )
    g_key_bf = (
        rotate_back(key_sum.reshape(row_count, KV, HD), cos_table, sin_table)
        .reshape(row_count, KV * HD)
        .astype(jnp.bfloat16)
    )
    g_value_bf = value_sum.astype(jnp.bfloat16)
    g_q_w = transposed_product(attn_in, g_query_bf)
    g_k_w = transposed_product(attn_in, g_key_bf)
    g_v_w = transposed_product(attn_in, g_value_bf)
    g_attn_in = (
        jnp.einsum("tn,kn->tk", g_query_bf, q_w, preferred_element_type=jnp.float32)
        + jnp.einsum("tn,kn->tk", g_key_bf, k_w, preferred_element_type=jnp.float32)
        + jnp.einsum("tn,kn->tk", g_value_bf, v_w, preferred_element_type=jnp.float32)
    )
    g_attn_gain = jnp.sum(g_attn_in * normed, axis=0)
    g_hidden = g_middle + rms_back(g_attn_in, normed, factor, attn_g)
    terms = (g_attn_gain, g_q_w, g_k_w, g_v_w, g_o_w, g_ffn_gain, g_gate_w, g_up_w, g_down)
    return (g_hidden, terms)


def share_terms(terms):
    return (
        lax.psum_scatter(terms[0], "shard", scatter_dimension=0, tiled=True),
        lax.psum_scatter(terms[1], "shard", scatter_dimension=0, tiled=True),
        lax.psum_scatter(terms[2], "shard", scatter_dimension=0, tiled=True),
        lax.psum_scatter(terms[3], "shard", scatter_dimension=0, tiled=True),
        lax.psum_scatter(terms[4], "shard", scatter_dimension=0, tiled=True),
        lax.psum_scatter(terms[5], "shard", scatter_dimension=0, tiled=True),
        lax.psum_scatter(terms[6], "shard", scatter_dimension=0, tiled=True),
        lax.psum_scatter(terms[7], "shard", scatter_dimension=0, tiled=True),
        lax.psum_scatter(terms[8], "shard", scatter_dimension=0, tiled=True),
    )


def replica_sum(shares):
    return lax.psum(
        (
            shares[0],
            shares[1],
            shares[2],
            shares[3],
            shares[4],
            shares[5],
            shares[6],
            shares[7],
            shares[8],
        ),
        "rep",
    )


def body(
    tokens,
    block_order,
    attn_gain,
    q_weight,
    k_weight,
    v_weight,
    o_weight,
    ffn_gain,
    gate_weight,
    up_weight,
    down_weight,
    cotangent,
):
    row_count = tokens.shape[0]
    order_row = block_order[0]
    own_block = lax.dynamic_index_in_dim(order_row, lax.axis_index("shard"), 0, keepdims=False)
    local_index = jnp.arange(row_count, dtype=jnp.int32)
    q_positions = own_block * row_count + local_index
    key_positions = (order_row[:, None] * row_count + local_index[None, :]).reshape(-1)
    cos_table, sin_table = rope_tables(q_positions, HD)
    params = (
        attn_gain,
        q_weight,
        k_weight,
        v_weight,
        o_weight,
        ffn_gain,
        gate_weight,
        up_weight,
        down_weight,
    )
    hidden = tokens.astype(jnp.float32)
    kept_weights = []
    layer_index = 0
    gathered = gather_forward(params, layer_index)
    hidden, saved = layer_forward(
        hidden, gathered, q_positions, key_positions, cos_table, sin_table
    )
    saved_list = [saved]
    kept_weights.append(gathered)
    gradient = cotangent.astype(jnp.float32)
    reduced = [None] * LAYERS
    for layer_index in reversed(range(LAYERS)):
        gathered = gather_backward(params, layer_index)
        gradient, terms = layer_backward(
            gradient,
            saved_list[layer_index],
            gathered,
            q_positions,
            key_positions,
            cos_table,
            sin_table,
        )
        shares = replica_sum(share_terms(terms))
        reduced[layer_index] = shares
    stacked = tuple((jnp.stack([reduced[0][member]]) for member in range(9)))
    return (
        hidden,
        gradient,
        stacked[0],
        stacked[1],
        stacked[2],
        stacked[3],
        stacked[4],
        stacked[5],
        stacked[6],
        stacked[7],
        stacked[8],
    )


F32 = jnp.float32
BF16 = jnp.bfloat16
MESH = pl.DeviceIdType.MESH


def nn(left, right):
    return lax.dot_general(left, right, (((1,), (0,)), ((), ())), preferred_element_type=F32)


def nt(left, right):
    return lax.dot_general(left, right, (((1,), (1,)), ((), ())), preferred_element_type=F32)


def tn(left, right):
    return lax.dot_general(left, right, (((0,), (0,)), ((), ())), preferred_element_type=F32)


def swap_halves(x):
    width = x.shape[-1]
    lane = lax.broadcasted_iota(jnp.int32, x.shape, 1)
    return jnp.where(
        lane % HD < HD // 2, pltpu.roll(x, width - HD // 2, 1), pltpu.roll(x, HD // 2, 1)
    )


def fused_kernel(
    tok_hbm, order_ref, again_ref, q_hbm, k_hbm, v_hbm, o_hbm, fgain_ref, gate_hbm, up_hbm, down_hbm,
    cot_hbm,
    out_ref, gin_ref, o1_ref, o2_ref, o3_ref,
    tok_ref, cot_ref, down_ref, w5, w1, wg, wu, gain_ref, gain_in, cot, kv, bb, part_out, part_in, dbo, dbi, probs, a_half, t_half, dm_x,
    dkv_out, dkv_in, dqk_x, dv_x, gg_out, gg_in, g1, g2, g3, r1a, r1b, r1c, r2a, r2b, r2c,
    r3a, r3b, r3c, f1, f2, f3, send_sem, recv_sem, local_sem,
):
    rows = tok_ref.shape[0]
    rep = lax.axis_index("rep")
    s = lax.axis_index("shard")
    core = rep % 2
    y = (rep // 2) % 2
    z = rep // 4
    xpeer = (rep, 1 - s)
    cpeer = (rep + 1 - 2 * core, s)
    ypeer = (rep + 2 - 4 * y, s)

    def zdev(z2):
        return (z2 * 4 + y * 2 + core, s)

    zpeers = [zdev((z + d) % 4) for d in (1, 2, 3)]
    counter = [0]
    started = []

    def remote(src, dst, device):
        i = counter[0]
        counter[0] += 1
        c = pltpu.make_async_remote_copy(
            src_ref=src, dst_ref=dst, send_sem=send_sem.at[i], recv_sem=recv_sem.at[i],
            device_id=device, device_id_type=MESH,
        )
        c.start()
        started.append(c)
        return c

    gate_ref, up_ref = gate_hbm.at[0], up_hbm.at[0]
    half = gate_ref.shape[0]
    ffh = wg.shape[1]
    mine = pl.multiple_of(s * half, 16)
    theirs = pl.multiple_of((1 - s) * half, 16)
    ffcols = pl.ds(pl.multiple_of(s * ffh, 128), ffh)
    own_rows = pl.ds(mine, half)
    pairs = [
        (q_hbm.at[0], w5.at[0, own_rows]), (o_hbm.at[0], w5.at[1, own_rows]),
        (k_hbm.at[0], w1.at[0, own_rows]), (v_hbm.at[0], w1.at[1, own_rows]),
        (tok_hbm, tok_ref), (cot_hbm, cot_ref), (gate_ref.at[:, ffcols], wg.at[own_rows]),
        (up_ref.at[:, ffcols], wu.at[own_rows]), (down_hbm.at[0], down_ref),
    ]
    local = [
        pltpu.make_async_copy(src, dst, local_sem.at[i]) for i, (src, dst) in enumerate(pairs)
    ]
    for c in local:
        c.start()

    lane = lax.broadcasted_iota(jnp.int32, (rows, 128), 1)
    sub = lax.broadcasted_iota(jnp.int32, (rows, 128), 0)
    own, other = order_ref[0, s], order_ref[0, 1 - s]
    position = own * rows + sub
    frequency = jnp.exp((lane % (HD // 2)).astype(F32) * (-2.0 * math.log(rope_base) / HD))
    angle = position.astype(F32) * frequency
    cos_t = jnp.cos(angle)
    sin_t = jnp.sin(angle)
    sin_t = jnp.where(lane % HD < HD // 2, -sin_t, sin_t)
    cos_t = jnp.concatenate([cos_t] * 6, axis=1)
    sin_t = jnp.concatenate([sin_t] * 6, axis=1)
    bias = jnp.concatenate(
        [
            jnp.where(start * rows + lane <= position, 0.0, -1e30).astype(F32)
            for start in (own, other)
        ],
        axis=1,
    )
    both = jnp.concatenate([again_ref[...], fgain_ref[...]], axis=0).astype(F32)
    none = jnp.zeros_like(both)
    gain_ref[0:2] = jnp.where(
        s == 0,
        jnp.concatenate([both, none], axis=1),
        jnp.concatenate([none, both], axis=1),
    )
    gain_ref[2:8] = jnp.zeros((6, 2 * half), F32)

    barrier = pltpu.get_barrier_semaphore()
    for peer in [xpeer, cpeer, ypeer] + zpeers:
        pl.semaphore_signal(barrier, inc=1, device_id=peer, device_id_type=MESH)
    pl.semaphore_wait(barrier, 6)

    gain_copy = remote(gain_ref, gain_in, xpeer)
    for c in local[:4]:
        c.wait()
    hr = half // 2
    rows_x = pl.ds(pl.multiple_of(s * half + y * hr, 16), hr)
    rows_y = pl.ds(pl.multiple_of(theirs + y * hr, 16), hr)
    part_x = pl.ds(pl.multiple_of(y * hr, 16), hr)
    hc = ffh // 2
    cols = pl.ds(pl.multiple_of(core * hc, 128), hc)
    cols_x = pl.ds(pl.multiple_of((1 - s) * ffh + core * hc, 128), hc)

    def send(block, device):
        return remote(block, block, device)

    x5 = send(w5.at[core, rows_x], xpeer)
    x1 = send(w1.at[core, rows_x], xpeer)
    local[5].wait()
    xg = remote(gate_ref.at[part_x, cols_x], wg.at[rows_x, cols], xpeer)
    xu = remote(up_ref.at[part_x, cols_x], wu.at[rows_x, cols], xpeer)
    cot_copy = remote(cot_ref, cot, xpeer)
    rows_c = pl.ds(theirs, half)

    def forward(copy, block, device):
        copy.wait_recv()
        return send(block, device)

    y5 = forward(x5, w5.at[core, rows_y], ypeer)
    y1 = forward(x1, w1.at[core, rows_y], ypeer)
    local[4].wait()
    hidden = tok_ref[...].astype(F32)
    rr = lax.rsqrt(jnp.mean(hidden * hidden, axis=-1, keepdims=True) + norm_eps)
    normed = hidden * rr
    gain_copy.wait_recv()
    gains = gain_ref[...] + gain_in[...]
    attn_g = gains[0:1, :]
    ffn_g = gains[1:2, :]
    attn_in = (normed * attn_g).astype(BF16)
    c5 = forward(y5, w5.at[core, rows_c], cpeer)
    c1 = forward(y1, w1.at[core, rows_c], cpeer)
    yg = forward(xg, wg.at[rows_y, cols], ypeer)
    yu = forward(xu, wu.at[rows_y, cols], ypeer)
    dm = attn_in.shape[1] // 2

    def pick(value, flag):
        return jnp.where(flag == 0, value[:, :dm], value[:, dm:])

    c5.wait_recv()
    c1.wait_recv()
    qk = jnp.concatenate([nn(attn_in, w5[0]), nn(attn_in, w1[0])], axis=1)
    qk = (qk * cos_t + swap_halves(qk) * sin_t).astype(BF16)
    v = nn(attn_in, w1[1]).astype(BF16)
    kv_own = jnp.concatenate([qk[:, 576:768], v], axis=1)
    kv[0] = kv_own
    kv_copy = remote(kv.at[0], kv.at[1], xpeer)
    a_half[0] = pick(attn_in, s)
    a_half[1] = pick(attn_in, 1 - s)
    cg = forward(yg, wg.at[rows_c, cols], cpeer)
    cu = forward(yu, wu.at[rows_c, cols], cpeer)
    kv_copy.wait_recv()
    kv_oth = kv[1]
    groups = H // KV
    bias3 = jnp.concatenate([bias] * groups, axis=0)

    def stack(value, g):
        return jnp.concatenate(
            [value[:, HD * j : HD * (j + 1)] for j in range(g * groups, (g + 1) * groups)], axis=0
        )

    def unstack(values):
        return [v[i * rows : (i + 1) * rows] for v in values for i in range(groups)]

    def keys(off, g):
        lo = off + HD * g
        return jnp.concatenate([kv_own[:, lo : lo + HD], kv_oth[:, lo : lo + HD]], axis=0)

    qs = [stack(qk, g) for g in range(KV)]
    ks = [keys(0, g) for g in range(KV)]
    vs = [keys(KV * HD, g) for g in range(KV)]
    outs = []
    for g in range(KV):
        sc = nt(qs[g], ks[g]) * HD ** (-0.5) + bias3
        top = jnp.max(sc, axis=-1, keepdims=True)
        lse = top + jnp.log(jnp.sum(jnp.exp(sc - top), axis=-1, keepdims=True))
        p = jnp.exp(sc - lse)
        probs[g] = p
        outs.append(nn(p.astype(BF16), vs[g]).astype(BF16))
    attended = jnp.concatenate(unstack(outs), axis=1)
    w_o = w5[1]
    middle = hidden + nn(attended, w_o)
    rr2 = lax.rsqrt(jnp.mean(middle * middle, axis=-1, keepdims=True) + norm_eps)
    normed2 = middle * rr2
    bb[0:rows] = (normed2 * ffn_g).astype(BF16)
    b_copy = remote(bb.at[pl.ds(0, rows)], bb.at[pl.ds(rows, rows)], xpeer)
    t_half[0] = pick(attended, s)
    t_half[1] = pick(attended, 1 - s)
    a_copy = remote(a_half.at[1], a_half.at[2], xpeer)
    for c in local[6:]:
        c.wait()
    cot_copy.wait_recv()
    grad_all = jnp.concatenate([cot_ref[...], cot[...]], axis=0)
    d_mix = nt(grad_all, down_ref[...])
    cg.wait_recv()
    cu.wait_recv()
    b_copy.wait_recv()
    ball = bb[...]
    gt = nn(ball, wg[...])
    up = nn(ball, wu[...])
    sig = jax.nn.sigmoid(gt)
    silu = gt * sig
    mix = (silu * up).astype(BF16)
    d_up = (d_mix * silu).astype(BF16)
    d_gt = (d_mix * up * sig * (1.0 + gt * (1.0 - sig))).astype(BF16)
    db = nt(d_gt, wg[...]) + nt(d_up, wu[...])
    dbo[...] = db[rows:].astype(BF16)
    db_copy = remote(dbo, dbi, xpeer)
    part = nn(mix, down_ref[...])
    part_out[...] = part[rows:].astype(BF16)
    part_copy = remote(part_out, part_in, xpeer)
    t_copy = remote(t_half.at[1], t_half.at[2], xpeer)

    gs, r1, r2, r3 = (g2, g1, g3), (r1b, r1a, r1c), (r2b, r2a, r2c), (r3b, r3a, r3c)
    fs, res = (f2, f1, f3), (o2_ref, o1_ref, o3_ref)
    state = [None] * 3

    def rs_core(p):
        state[p] = remote(gs[p].at[pl.ds((1 - core) * 8, 8)], r1[p], cpeer)

    def rs_y(p):
        state[p].wait_recv()

        @pl.loop(0, 8)
        def _(k):
            r1[p][k] = (r1[p][k].astype(F32) + gs[p][core * 8 + k].astype(F32)).astype(BF16)

        state[p] = remote(r1[p].at[pl.ds((1 - y) * 4, 4)], r2[p], ypeer)

    def rs_z(p):
        state[p].wait_recv()

        @pl.loop(0, 4)
        def _(k):
            r2[p][k] = (r2[p][k].astype(F32) + r1[p][y * 4 + k].astype(F32)).astype(BF16)

        state[p] = [
            remote(r2[p].at[(z + d) % 4], r3[p].at[d - 1], zpeers[d - 1]) for d in (1, 2, 3)
        ]

    def ag_z(p):
        for c in state[p]:
            c.wait_recv()
        total = r2[p][z].astype(F32)
        for d in range(3):
            total = total + r3[p][d].astype(F32)
        slot = core
        if p == 1:
            fs[p][0] = total.astype(BF16)
            i = counter[0]
            counter[0] += 1
            swap = pltpu.make_async_remote_copy(
                src_ref=fs[p].at[0], dst_ref=fs[p].at[1], send_sem=send_sem.at[i],
                recv_sem=recv_sem.at[i], device_id=xpeer, device_id_type=MESH,
            )

            @pl.when(core == 1)
            def _():
                swap.start()
                swap.wait()
                fs[p][0] = fs[p][1]

            slot = jnp.where(s == 0, core, 1 - core)
            res[p][slot * 8 + y * 4 + z] = fs[p][0]
        else:
            fs[p][0] = total.astype(BF16)
            res[p][slot * 8 + y * 4 + z] = fs[p][0]
        place = slot * 8 + y * 4 + z
        state[p] = [
            remote(fs[p].at[0], res[p].at[place], zpeers[d - 1]) for d in (1, 2, 3)
        ]
        return slot

    slots = [None] * 3

    def ag_y(p):
        for c in state[p]:
            c.wait_recv()
        block = res[p].at[pl.ds(slots[p] * 8 + y * 4, 4)]
        state[p] = remote(block, block, ypeer)

    def ag_core(p):
        state[p].wait_recv()
        block = res[p].at[pl.ds(slots[p] * 8, 8)]
        state[p] = remote(block, block, cpeer)

    g2[...] = tn(mix, grad_all).astype(BF16).reshape(g2.shape)
    rs_core(0)
    for half_t, dd in enumerate((d_gt, d_up)):
        gw = tn(ball, dd).astype(BF16)
        for h in range(2):
            for yy in range(2):
                for zz in range(2):
                    k = jnp.where(s == h, 0, 8) + yy * 4 + half_t * 2 + zz
                    lo = h * half + yy * hr
                    g1[k] = gw[lo : lo + hr, zz * 384 : (zz + 1) * 384]
    rs_core(1)
    db_copy.wait_recv()
    db = db[:rows] + dbi[...].astype(F32)
    gain2 = jnp.sum(db * normed2, axis=0, keepdims=True)
    e = db * ffn_g
    dm1 = cot_ref[...].astype(F32) + rr2 * (
        e - normed2 * jnp.mean(e * normed2, axis=-1, keepdims=True)
    )
    dm1b = dm1.astype(BF16)
    dm_x[0] = dm1b
    dm_copy = remote(dm_x.at[0], dm_x.at[1], xpeer)
    d_att = nt(dm1b, w_o).astype(BF16)
    rs_y(0)
    part_copy.wait_recv()
    out_ref[...] = middle + part[:rows] + part_in[...].astype(F32)

    dqs, dks, dvs = [], [], []
    for g in range(KV):
        do_g = stack(d_att, g)
        p = probs[g]
        dvs.append(tn(p.astype(BF16), do_g))
        delta = jnp.sum(do_g.astype(F32) * outs[g].astype(F32), axis=-1, keepdims=True)
        ds = (p * (nt(do_g, vs[g]) - delta) * HD ** (-0.5)).astype(BF16)
        dqs.append(nn(ds, ks[g]))
        dks.append(tn(ds, qs[g]))
        if g == 0:
            rs_y(1)
    dkv = jnp.concatenate(dks + dvs, axis=1)
    dkv_out[...] = dkv[rows:].astype(BF16)
    dkv_copy = remote(dkv_out, dkv_in, xpeer)
    rs_z(0)
    dkv_copy.wait_recv()
    dkv = dkv[:rows] + dkv_in[...].astype(F32)
    dqk = jnp.concatenate(unstack(dqs) + [dkv[:, : KV * HD]], axis=1)
    dqk = (dqk * cos_t - swap_halves(dqk) * sin_t).astype(BF16)
    dvb = dkv[:, KV * HD :].astype(BF16)
    dqk_x[0] = dqk
    dv_x[0] = dvb
    dqk_copy = remote(dqk_x.at[0], dqk_x.at[1], xpeer)
    dv_copy = remote(dv_x.at[0], dv_x.at[1], xpeer)
    da = nt(dqk[:, :576], w5[0]) + nt(dqk[:, 576:], w1[0]) + nt(dvb, w1[1])
    gain1 = jnp.sum(da * normed, axis=0, keepdims=True)
    gg_out[...] = jnp.concatenate([gain1, gain2, jnp.zeros((6, gain1.shape[1]), F32)], axis=0)
    gg_copy = remote(gg_out, gg_in, xpeer)
    rs_z(1)
    f = da * attn_g
    gin_ref[...] = dm1 + rr * (f - normed * jnp.mean(f * normed, axis=-1, keepdims=True))
    for c in (a_copy, t_copy, dm_copy, dqk_copy, dv_copy):
        c.wait_recv()
    a_all = jnp.concatenate([a_half[0], a_half[2]], axis=0)
    t_all = jnp.concatenate([t_half[0], t_half[2]], axis=0)
    gw_o = tn(t_all, jnp.concatenate([dm_x[0], dm_x[1]], axis=0)).astype(BF16)
    gw_qk = tn(a_all, jnp.concatenate([dqk_x[0], dqk_x[1]], axis=0)).astype(BF16)
    gw_v = tn(a_all, jnp.concatenate([dv_x[0], dv_x[1]], axis=0)).astype(BF16)
    columns = [
        gw_qk[:, :384], gw_qk[:, 384:], gw_o[:, :384],
        jnp.concatenate([gw_o[:, 384:], gw_v], axis=1),
    ]
    gg_copy.wait_recv()
    gg = pick(gg_out[...] + gg_in[...], s)
    gg = jnp.concatenate([gg, jnp.zeros((8, 384 - dm), F32)], axis=1)
    row32 = lax.broadcasted_iota(jnp.int32, (32, 384), 0)
    for cc in range(4):
        for r in range(3):
            g3[r * 4 + cc] = columns[cc][r * 80 : (r + 1) * 80]
        g3[12 + cc, 0:48] = columns[cc][240:288]
        if cc < 2:
            tail = jnp.where(row32 == 0, jnp.broadcast_to(gg[cc : cc + 1], (32, 384)), 0.0)
        else:
            tail = jnp.zeros((32, 384), F32)
        g3[12 + cc, 48:80] = tail.astype(BF16)
    rs_core(2)
    slots[0] = ag_z(0)
    rs_y(2)
    slots[1] = ag_z(1)
    rs_z(2)
    ag_y(0)
    slots[2] = ag_z(2)
    ag_y(1)
    ag_core(0)
    ag_y(2)
    ag_core(1)
    ag_core(2)
    for st in state:
        st.wait_recv()
    for c in started:
        c.wait_send()


def unpack_kernel(
    b_ref, i_ref, o1_ref, o2_ref, o3_ref,
    block_ref, gin_ref, ag_ref, q_ref, k_ref, v_ref, o_ref, fg_ref, gate_ref, up_ref, down_ref,
):
    block_ref[...] = b_ref[...]
    gin_ref[...] = i_ref[...]
    half = ag_ref.shape[1]
    ffh = gate_ref.shape[2] // 2
    for f in range(2):
        for yy in range(2):
            for t, ref in enumerate((gate_ref, up_ref)):
                for zz in range(2):
                    lo = f * ffh + zz * 384
                    ref[0, yy * 144 : (yy + 1) * 144, lo : lo + 384] = o1_ref[
                        f * 8 + yy * 4 + t * 2 + zz
                    ].astype(F32)
    down_ref[0] = o2_ref[...].reshape(down_ref.shape[1:]).astype(F32)
    for r in range(4):
        lo = r * 80
        n = 80 if r < 3 else 48
        rows = slice(lo, lo + n)
        q_ref[0, rows, :384] = o3_ref[r * 4, :n].astype(F32)
        mid = o3_ref[r * 4 + 1, :n].astype(F32)
        q_ref[0, rows, 384:] = mid[:, :192]
        k_ref[0, rows] = mid[:, 192:]
        o_ref[0, rows, :384] = o3_ref[r * 4 + 2, :n].astype(F32)
        last = o3_ref[r * 4 + 3, :n].astype(F32)
        o_ref[0, rows, 384:] = last[:, :192]
        v_ref[0, rows] = last[:, 192:]
    ag_ref[...] = o3_ref[12, 48:64].astype(F32)[0:1, :half]
    fg_ref[...] = o3_ref[13, 48:64].astype(F32)[0:1, :half]


def fused_body(
    tokens, block_order, attn_gain, q_weight, k_weight, v_weight, o_weight, ffn_gain,
    gate_weight, up_weight, down_weight, cotangent,
):
    rows, width = tokens.shape
    half = attn_gain.shape[1]
    ff = gate_weight.shape[2]
    vm = pl.BlockSpec(memory_space=pltpu.VMEM)
    hbm = pl.BlockSpec(memory_space=pl.ANY)
    shapes = [(144, 384), (48, width), (80, 384)]

    def buf(*shape, dtype=BF16):
        return pltpu.VMEM(shape, dtype)

    scratch = [
        buf(rows, width), buf(rows, width), buf(ff // 2, width), buf(2, width, width),
        buf(2, width, KV * HD), buf(width, ff // 2), buf(width, ff // 2),
        buf(8, width, dtype=F32), buf(8, width, dtype=F32),
        buf(rows, width), buf(2, rows, 384), buf(2 * rows, width), buf(rows, width),
        buf(rows, width), buf(rows, width), buf(rows, width),
        buf(KV, 3 * rows, 2 * rows, dtype=F32), buf(3, rows, half), buf(3, rows, half),
        buf(2, rows, width), buf(rows, 384), buf(rows, 384), buf(2, rows, 768),
        buf(2, rows, 192), buf(8, width, dtype=F32), buf(8, width, dtype=F32),
    ]
    for count in (16, 8, 4, 3, 2):
        scratch += [buf(count, *sh) for sh in shapes]
    scratch += [
        pltpu.SemaphoreType.DMA((64,)), pltpu.SemaphoreType.DMA((64,)),
        pltpu.SemaphoreType.DMA((9,)),
    ]
    block_out, input_grad, o1, o2, o3 = pl.pallas_call(
        fused_kernel,
        out_shape=(
            jax.ShapeDtypeStruct((rows, width), F32),
            jax.ShapeDtypeStruct((rows, width), F32),
            *[jax.ShapeDtypeStruct((16, *sh), BF16) for sh in shapes],
        ),
        in_specs=[
            hbm, pl.BlockSpec(memory_space=pltpu.SMEM), vm, *[hbm] * 4, vm, *[hbm] * 4,
        ],
        out_specs=[vm] * 5,
        scratch_shapes=scratch,
        compiler_params=pltpu.CompilerParams(
            collective_id=0, has_side_effects=True, vmem_limit_bytes=56 * 1024 * 1024
        ),
    )(
        tokens, block_order, attn_gain, q_weight, k_weight, v_weight, o_weight, ffn_gain,
        gate_weight, up_weight, down_weight, cotangent,
    )
    shapes = [
        (rows, width), (rows, width), (1, half), (1, half, width), (1, half, KV * HD),
        (1, half, KV * HD), (1, half, width), (1, half), (1, half, ff), (1, half, ff),
        (1, ff // 2, width),
    ]
    return pl.pallas_call(
        unpack_kernel,
        out_shape=tuple(jax.ShapeDtypeStruct(shape, F32) for shape in shapes),
        in_specs=[vm] * 5,
        out_specs=(vm,) * 11,
        compiler_params=pltpu.CompilerParams(vmem_limit_bytes=40 * 1024 * 1024),
    )(block_out, input_grad, o1, o2, o3)


def solution(mesh):
    placed = (
        P(("rep", "shard"), None),
        P("rep", None),
        P(None, "shard"),
        P(None, "shard", None),
        P(None, "shard", None),
        P(None, "shard", None),
        P(None, "shard", None),
        P(None, "shard"),
        P(None, "shard", None),
        P(None, "shard", None),
        P(None, "shard", None),
        P(("rep", "shard"), None),
    )
    fused = mesh.shape["shard"] == 2 and mesh.shape["rep"] == 16
    return jax.shard_map(
        fused_body if fused else body,
        mesh=mesh,
        in_specs=placed,
        out_specs=(
            P(("rep", "shard"), None),
            P(("rep", "shard"), None),
            P(None, "shard"),
            P(None, "shard", None),
            P(None, "shard", None),
            P(None, "shard", None),
            P(None, "shard", None),
            P(None, "shard"),
            P(None, "shard", None),
            P(None, "shard", None),
            P(None, "shard", None),
        ),
        check_vma=False,
    )
```

```python
import math

import jax
import jax.numpy as jnp
from jax import lax
from jax.experimental import pallas as pl
from jax.experimental.pallas import tpu as pltpu
from jax.sharding import PartitionSpec as P

H = 9
KV = 3
HD = 64
LAYERS = 1


rope_base = 100000.0
norm_eps = 1e-05


def rope_tables(positions, head_dim):
    half_dim = head_dim // 2
    frequency = jnp.exp(
        jnp.arange(half_dim, dtype=jnp.float32) * (-2.0 * math.log(rope_base) / head_dim)
    )
    angles = positions.astype(jnp.float32)[:, None] * frequency[None, :]
    return (jnp.cos(angles)[:, None, :], jnp.sin(angles)[:, None, :])


def rotate(tensor, cos_table, sin_table):
    half_dim = tensor.shape[-1] // 2
    first_half = tensor[..., :half_dim]
    second_half = tensor[..., half_dim:]
    return jnp.concatenate(
        [
            first_half * cos_table - second_half * sin_table,
            second_half * cos_table + first_half * sin_table,
        ],
        axis=-1,
    )


def rotate_back(tensor, cos_table, sin_table):
    half_dim = tensor.shape[-1] // 2
    first_half = tensor[..., :half_dim]
    second_half = tensor[..., half_dim:]
    return jnp.concatenate(
        [
            first_half * cos_table + second_half * sin_table,
            second_half * cos_table - first_half * sin_table,
        ],
        axis=-1,
    )


def rms_scale(hidden):
    factor = lax.rsqrt(jnp.mean(hidden * hidden, axis=-1, keepdims=True) + norm_eps)
    return (hidden * factor, factor)


def rms_back(grad_in, normed, factor, gain_row):
    scaled = grad_in * gain_row.astype(jnp.float32)
    return factor * (scaled - normed * jnp.mean(scaled * normed, axis=-1, keepdims=True))


def transposed_product(left, right):
    return jnp.einsum("tk,tn->kn", left, right, preferred_element_type=jnp.float32)


def gather_forward(params, layer_index):
    return (
        lax.all_gather(params[0][layer_index], "shard", axis=0, tiled=True),
        lax.all_gather(params[1][layer_index], "shard", axis=0, tiled=True),
        lax.all_gather(params[2][layer_index], "shard", axis=0, tiled=True),
        lax.all_gather(params[3][layer_index], "shard", axis=0, tiled=True),
        lax.all_gather(params[4][layer_index], "shard", axis=0, tiled=True),
        lax.all_gather(params[5][layer_index], "shard", axis=0, tiled=True),
        lax.all_gather(params[6][layer_index], "shard", axis=0, tiled=True),
        lax.all_gather(params[7][layer_index], "shard", axis=0, tiled=True),
        lax.all_gather(params[8][layer_index], "shard", axis=0, tiled=True),
    )


def gather_backward(params, layer_index):
    return (
        lax.all_gather(params[0][layer_index], "shard", axis=0, tiled=True),
        lax.all_gather(params[1][layer_index], "shard", axis=0, tiled=True),
        lax.all_gather(params[2][layer_index], "shard", axis=0, tiled=True),
        lax.all_gather(params[3][layer_index], "shard", axis=0, tiled=True),
        lax.all_gather(params[4][layer_index], "shard", axis=0, tiled=True),
        lax.all_gather(params[5][layer_index], "shard", axis=0, tiled=True),
        lax.all_gather(params[6][layer_index], "shard", axis=0, tiled=True),
        lax.all_gather(params[7][layer_index], "shard", axis=0, tiled=True),
        lax.all_gather(params[8][layer_index], "shard", axis=0, tiled=True),
    )


def visible_scores(query_grouped, all_keys, q_positions, key_positions):
    scores = jnp.einsum(
        "sgmd,tgd->gmst", query_grouped, all_keys, preferred_element_type=jnp.float32
    ) * HD ** (-0.5)
    allowed = key_positions[None, :] <= q_positions[:, None]
    return (jnp.where(allowed, scores, -1e30), allowed)


def layer_forward(hidden, gathered, q_positions, key_positions, cos_table, sin_table):
    attn_g, q_w, k_w, v_w, o_w, ffn_g, gate_w, up_w, down_w = gathered
    row_count = hidden.shape[0]
    head_groups = H // KV
    normed, factor = rms_scale(hidden)
    attn_in = (normed * attn_g.astype(jnp.float32)).astype(jnp.bfloat16)
    query_rows = rotate(
        jnp.dot(attn_in, q_w, preferred_element_type=jnp.float32).reshape(row_count, H, HD),
        cos_table,
        sin_table,
    ).astype(jnp.bfloat16)
    key_rows = rotate(
        jnp.dot(attn_in, k_w, preferred_element_type=jnp.float32).reshape(row_count, KV, HD),
        cos_table,
        sin_table,
    ).astype(jnp.bfloat16)
    value_rows = jnp.dot(attn_in, v_w, preferred_element_type=jnp.float32).astype(jnp.bfloat16)
    all_keys, all_values = (
        lax.all_gather(key_rows.reshape(row_count, KV * HD), "shard", axis=0, tiled=True),
        lax.all_gather(value_rows, "shard", axis=0, tiled=True),
    )
    all_keys = all_keys.reshape(-1, KV, HD)
    all_values = all_values.reshape(-1, KV, HD)
    query_grouped = query_rows.reshape(row_count, KV, head_groups, HD)
    scores, allowed = visible_scores(query_grouped, all_keys, q_positions, key_positions)
    row_max = jnp.max(scores, axis=-1, keepdims=True)
    row_total = jnp.sum(jnp.exp(scores - row_max), axis=-1, keepdims=True)
    log_total = (row_max + jnp.log(row_total))[..., 0]
    probs_bf = jnp.where(allowed, jnp.exp(scores - log_total[..., None]), 0.0).astype(jnp.bfloat16)
    attended = (
        jnp.einsum("gmst,tgd->sgmd", probs_bf, all_values, preferred_element_type=jnp.float32)
        .astype(jnp.bfloat16)
        .reshape(row_count, H * HD)
    )
    middle = hidden + jnp.dot(attended, o_w, preferred_element_type=jnp.float32)
    normed_two, factor_two = rms_scale(middle)
    ffn_in = (normed_two * ffn_g.astype(jnp.float32)).astype(jnp.bfloat16)
    gate_pre = jnp.dot(ffn_in, gate_w, preferred_element_type=jnp.float32)
    up_pre = jnp.dot(ffn_in, up_w, preferred_element_type=jnp.float32)
    mixed = (jax.nn.silu(gate_pre) * up_pre).astype(jnp.bfloat16)
    output = middle + jnp.dot(mixed, down_w, preferred_element_type=jnp.float32)
    saved = (
        normed,
        factor,
        attn_in,
        query_grouped,
        all_keys,
        all_values,
        log_total,
        attended,
        normed_two,
        factor_two,
        ffn_in,
        gate_pre,
        up_pre,
        mixed,
    )
    return (output, saved)


def layer_backward(gradient, saved, gathered, q_positions, key_positions, cos_table, sin_table):
    attn_g, q_w, k_w, v_w, o_w, ffn_g, gate_w, up_w, down_w = gathered
    (
        normed,
        factor,
        attn_in,
        query_grouped,
        all_keys,
        all_values,
        log_total,
        attended,
        normed_two,
        factor_two,
        ffn_in,
        gate_pre,
        up_pre,
        mixed,
    ) = saved
    row_count = gradient.shape[0]
    head_groups = H // KV
    grad_bf = gradient.astype(jnp.bfloat16)
    g_down = transposed_product(mixed, grad_bf)
    g_mixed = jnp.einsum("tn,kn->tk", grad_bf, down_w, preferred_element_type=jnp.float32)
    sigmoid_gate = jax.nn.sigmoid(gate_pre)
    g_up = (g_mixed * gate_pre * sigmoid_gate).astype(jnp.bfloat16)
    g_gate = (g_mixed * up_pre * sigmoid_gate * (1.0 + gate_pre * (1.0 - sigmoid_gate))).astype(
        jnp.bfloat16
    )
    g_gate_w = transposed_product(ffn_in, g_gate)
    g_up_w = transposed_product(ffn_in, g_up)
    g_ffn_in = jnp.einsum(
        "tn,kn->tk", g_gate, gate_w, preferred_element_type=jnp.float32
    ) + jnp.einsum("tn,kn->tk", g_up, up_w, preferred_element_type=jnp.float32)
    g_ffn_gain = jnp.sum(g_ffn_in * normed_two, axis=0)
    g_middle = gradient + rms_back(g_ffn_in, normed_two, factor_two, ffn_g)
    middle_bf = g_middle.astype(jnp.bfloat16)
    g_o_w = transposed_product(attended, middle_bf)
    g_attended = (
        jnp.einsum("tn,kn->tk", middle_bf, o_w, preferred_element_type=jnp.float32)
        .astype(jnp.bfloat16)
        .reshape(row_count, KV, head_groups, HD)
    )
    scores, allowed = visible_scores(query_grouped, all_keys, q_positions, key_positions)
    probs = jnp.where(allowed, jnp.exp(scores - log_total[..., None]), 0.0)
    probs_bf = probs.astype(jnp.bfloat16)
    value_terms = jnp.einsum(
        "gmst,sgmd->tgd", probs_bf, g_attended, preferred_element_type=jnp.float32
    )
    g_probs = jnp.einsum(
        "sgmd,tgd->gmst", g_attended, all_values, preferred_element_type=jnp.float32
    )
    delta = jnp.einsum(
        "sgmd,sgmd->gms",
        g_attended,
        attended.reshape(row_count, KV, head_groups, HD),
        preferred_element_type=jnp.float32,
    )
    g_scores = (probs * (g_probs - delta[..., None]) * HD ** (-0.5)).astype(jnp.bfloat16)
    g_query = jnp.einsum("gmst,tgd->sgmd", g_scores, all_keys, preferred_element_type=jnp.float32)
    key_terms = jnp.einsum(
        "gmst,sgmd->tgd", g_scores, query_grouped, preferred_element_type=jnp.float32
    )
    seq_rows = key_terms.shape[0]
    key_sum, value_sum = (
        lax.psum_scatter(
            key_terms.reshape(seq_rows, KV * HD), "shard", scatter_dimension=0, tiled=True
        ),
        lax.psum_scatter(
            value_terms.reshape(seq_rows, KV * HD), "shard", scatter_dimension=0, tiled=True
        ),
    )
    g_query_bf = (
        rotate_back(g_query.reshape(row_count, H, HD), cos_table, sin_table)
        .reshape(row_count, H * HD)
        .astype(jnp.bfloat16)
    )
    g_key_bf = (
        rotate_back(key_sum.reshape(row_count, KV, HD), cos_table, sin_table)
        .reshape(row_count, KV * HD)
        .astype(jnp.bfloat16)
    )
    g_value_bf = value_sum.astype(jnp.bfloat16)
    g_q_w = transposed_product(attn_in, g_query_bf)
    g_k_w = transposed_product(attn_in, g_key_bf)
    g_v_w = transposed_product(attn_in, g_value_bf)
    g_attn_in = (
        jnp.einsum("tn,kn->tk", g_query_bf, q_w, preferred_element_type=jnp.float32)
        + jnp.einsum("tn,kn->tk", g_key_bf, k_w, preferred_element_type=jnp.float32)
        + jnp.einsum("tn,kn->tk", g_value_bf, v_w, preferred_element_type=jnp.float32)
    )
    g_attn_gain = jnp.sum(g_attn_in * normed, axis=0)
    g_hidden = g_middle + rms_back(g_attn_in, normed, factor, attn_g)
    terms = (g_attn_gain, g_q_w, g_k_w, g_v_w, g_o_w, g_ffn_gain, g_gate_w, g_up_w, g_down)
    return (g_hidden, terms)


def share_terms(terms):
    return (
        lax.psum_scatter(terms[0], "shard", scatter_dimension=0, tiled=True),
        lax.psum_scatter(terms[1], "shard", scatter_dimension=0, tiled=True),
        lax.psum_scatter(terms[2], "shard", scatter_dimension=0, tiled=True),
        lax.psum_scatter(terms[3], "shard", scatter_dimension=0, tiled=True),
        lax.psum_scatter(terms[4], "shard", scatter_dimension=0, tiled=True),
        lax.psum_scatter(terms[5], "shard", scatter_dimension=0, tiled=True),
        lax.psum_scatter(terms[6], "shard", scatter_dimension=0, tiled=True),
        lax.psum_scatter(terms[7], "shard", scatter_dimension=0, tiled=True),
        lax.psum_scatter(terms[8], "shard", scatter_dimension=0, tiled=True),
    )


def replica_sum(shares):
    return lax.psum(
        (
            shares[0],
            shares[1],
            shares[2],
            shares[3],
            shares[4],
            shares[5],
            shares[6],
            shares[7],
            shares[8],
        ),
        "rep",
    )


def body(
    tokens,
    block_order,
    attn_gain,
    q_weight,
    k_weight,
    v_weight,
    o_weight,
    ffn_gain,
    gate_weight,
    up_weight,
    down_weight,
    cotangent,
):
    row_count = tokens.shape[0]
    order_row = block_order[0]
    own_block = lax.dynamic_index_in_dim(order_row, lax.axis_index("shard"), 0, keepdims=False)
    local_index = jnp.arange(row_count, dtype=jnp.int32)
    q_positions = own_block * row_count + local_index
    key_positions = (order_row[:, None] * row_count + local_index[None, :]).reshape(-1)
    cos_table, sin_table = rope_tables(q_positions, HD)
    params = (
        attn_gain,
        q_weight,
        k_weight,
        v_weight,
        o_weight,
        ffn_gain,
        gate_weight,
        up_weight,
        down_weight,
    )
    hidden = tokens.astype(jnp.float32)
    kept_weights = []
    layer_index = 0
    gathered = gather_forward(params, layer_index)
    hidden, saved = layer_forward(
        hidden, gathered, q_positions, key_positions, cos_table, sin_table
    )
    saved_list = [saved]
    kept_weights.append(gathered)
    gradient = cotangent.astype(jnp.float32)
    reduced = [None] * LAYERS
    for layer_index in reversed(range(LAYERS)):
        gathered = gather_backward(params, layer_index)
        gradient, terms = layer_backward(
            gradient,
            saved_list[layer_index],
            gathered,
            q_positions,
            key_positions,
            cos_table,
            sin_table,
        )
        shares = replica_sum(share_terms(terms))
        reduced[layer_index] = shares
    stacked = tuple((jnp.stack([reduced[0][member]]) for member in range(9)))
    return (
        hidden,
        gradient,
        stacked[0],
        stacked[1],
        stacked[2],
        stacked[3],
        stacked[4],
        stacked[5],
        stacked[6],
        stacked[7],
        stacked[8],
    )


F32 = jnp.float32
BF16 = jnp.bfloat16
MESH = pl.DeviceIdType.MESH


def nn(left, right):
    return lax.dot_general(left, right, (((1,), (0,)), ((), ())), preferred_element_type=F32)


def nt(left, right):
    return lax.dot_general(left, right, (((1,), (1,)), ((), ())), preferred_element_type=F32)


def tn(left, right):
    return lax.dot_general(left, right, (((0,), (0,)), ((), ())), preferred_element_type=F32)


def swap_halves(x):
    width = x.shape[-1]
    lane = lax.broadcasted_iota(jnp.int32, x.shape, 1)
    return jnp.where(
        lane % HD < HD // 2, pltpu.roll(x, width - HD // 2, 1), pltpu.roll(x, HD // 2, 1)
    )


def fused_kernel(
    tok_hbm, order_ref, again_ref, q_hbm, k_hbm, v_hbm, o_hbm, fgain_ref, gate_hbm, up_hbm, down_hbm,
    cot_hbm,
    out_ref, gin_ref, o1_ref, o2_ref, o3_ref,
    tok_t, cot_t, cot_ref, down_ref, w5, w1, wg, wu, gain_ref, gain_in, cot, kv, bb, part_out, part_in, dbo, dbi, probs, a_half, t_half, dm_x,
    dkv_out, dkv_in, dqk_x, dv_x, gg_out, gg_in, g1, g2, g3, r1a, r1b, r1c, r2a, r2b, r2c,
    r3a, r3b, r3c, f1, f2, f3, send_sem, recv_sem, local_sem,
):
    rows = tok_t.shape[1]
    rep = lax.axis_index("rep")
    s = lax.axis_index("shard")
    core = rep % 2
    y = (rep // 2) % 2
    z = rep // 4
    xpeer = (rep, 1 - s)
    cpeer = (rep + 1 - 2 * core, s)
    ypeer = (rep + 2 - 4 * y, s)

    def zdev(z2):
        return (z2 * 4 + y * 2 + core, s)

    zpeers = [zdev((z + d) % 4) for d in (1, 2, 3)]
    counter = [0]
    started = []

    def remote(src, dst, device):
        i = counter[0]
        counter[0] += 1
        c = pltpu.make_async_remote_copy(
            src_ref=src, dst_ref=dst, send_sem=send_sem.at[i], recv_sem=recv_sem.at[i],
            device_id=device, device_id_type=MESH,
        )
        c.start()
        started.append(c)
        return c

    gate_ref, up_ref = gate_hbm.at[0], up_hbm.at[0]
    half = gate_ref.shape[0]
    ffh = wg.shape[1]
    mine = pl.multiple_of(s * half, 16)
    theirs = pl.multiple_of((1 - s) * half, 16)
    ffcols = pl.ds(pl.multiple_of(s * ffh, 128), ffh)
    own_rows = pl.ds(mine, half)
    pairs = [
        (q_hbm.at[0], w5.at[0, own_rows]), (o_hbm.at[0], w5.at[1, own_rows]),
        (k_hbm.at[0], w1.at[0, own_rows]), (v_hbm.at[0], w1.at[1, own_rows]),
        (tok_hbm, tok_t), (cot_hbm, cot_t), (gate_ref.at[:, ffcols], wg.at[own_rows]),
        (up_ref.at[:, ffcols], wu.at[own_rows]), (down_hbm, down_ref),
    ]
    local = [
        pltpu.make_async_copy(src, dst, local_sem.at[i]) for i, (src, dst) in enumerate(pairs)
    ]
    for c in local:
        c.start()

    lane = lax.broadcasted_iota(jnp.int32, (rows, 128), 1)
    sub = lax.broadcasted_iota(jnp.int32, (rows, 128), 0)
    own, other = order_ref[0, s], order_ref[0, 1 - s]
    position = own * rows + sub
    frequency = jnp.exp((lane % (HD // 2)).astype(F32) * (-2.0 * math.log(rope_base) / HD))
    angle = position.astype(F32) * frequency
    cos_t = jnp.cos(angle)
    sin_t = jnp.sin(angle)
    sin_t = jnp.where(lane % HD < HD // 2, -sin_t, sin_t)
    cos_t = jnp.concatenate([cos_t] * 6, axis=1)
    sin_t = jnp.concatenate([sin_t] * 6, axis=1)
    bias = jnp.concatenate(
        [
            jnp.where(start * rows + lane <= position, 0.0, -1e30).astype(F32)
            for start in (own, other)
        ],
        axis=1,
    )
    both = jnp.concatenate([again_ref[...], fgain_ref[...]], axis=0).astype(F32)
    none = jnp.zeros_like(both)
    gain_ref[0:2] = jnp.where(
        s == 0,
        jnp.concatenate([both, none], axis=1),
        jnp.concatenate([none, both], axis=1),
    )
    gain_ref[2:8] = jnp.zeros((6, 2 * half), F32)

    local[5].wait()
    cot_ref[...] = cot_t[...].astype(F32).T.astype(BF16)
    barrier = pltpu.get_barrier_semaphore()
    for peer in [xpeer, cpeer, ypeer] + zpeers:
        pl.semaphore_signal(barrier, inc=1, device_id=peer, device_id_type=MESH)
    pl.semaphore_wait(barrier, 6)

    gain_copy = remote(gain_ref, gain_in, xpeer)
    for c in local[:4]:
        c.wait()
    hr = half // 2
    rows_x = pl.ds(pl.multiple_of(s * half + y * hr, 16), hr)
    rows_y = pl.ds(pl.multiple_of(theirs + y * hr, 16), hr)
    part_x = pl.ds(pl.multiple_of(y * hr, 16), hr)
    hc = ffh // 2
    cols = pl.ds(pl.multiple_of(core * hc, 128), hc)
    cols_x = pl.ds(pl.multiple_of((1 - s) * ffh + core * hc, 128), hc)

    def send(block, device):
        return remote(block, block, device)

    x5 = send(w5.at[core, rows_x], xpeer)
    x1 = send(w1.at[core, rows_x], xpeer)
    xg = remote(gate_ref.at[part_x, cols_x], wg.at[rows_x, cols], xpeer)
    xu = remote(up_ref.at[part_x, cols_x], wu.at[rows_x, cols], xpeer)
    cot_copy = remote(cot_ref, cot, xpeer)
    rows_c = pl.ds(theirs, half)

    def forward(copy, block, device):
        copy.wait_recv()
        return send(block, device)

    y5 = forward(x5, w5.at[core, rows_y], ypeer)
    y1 = forward(x1, w1.at[core, rows_y], ypeer)
    local[4].wait()
    hidden = tok_t[...].astype(F32).T
    rr = lax.rsqrt(jnp.mean(hidden * hidden, axis=-1, keepdims=True) + norm_eps)
    normed = hidden * rr
    gain_copy.wait_recv()
    gains = gain_ref[...] + gain_in[...]
    attn_g = gains[0:1, :]
    ffn_g = gains[1:2, :]
    attn_in = (normed * attn_g).astype(BF16)
    c5 = forward(y5, w5.at[core, rows_c], cpeer)
    c1 = forward(y1, w1.at[core, rows_c], cpeer)
    yg = forward(xg, wg.at[rows_y, cols], ypeer)
    yu = forward(xu, wu.at[rows_y, cols], ypeer)
    dm = attn_in.shape[1] // 2

    def pick(value, flag):
        return jnp.where(flag == 0, value[:, :dm], value[:, dm:])

    c5.wait_recv()
    c1.wait_recv()
    qk = jnp.concatenate([nn(attn_in, w5[0]), nn(attn_in, w1[0])], axis=1)
    qk = (qk * cos_t + swap_halves(qk) * sin_t).astype(BF16)
    v = nn(attn_in, w1[1]).astype(BF16)
    kv_own = jnp.concatenate([qk[:, 576:768], v], axis=1)
    kv[0] = kv_own
    kv_copy = remote(kv.at[0], kv.at[1], xpeer)
    a_half[0] = pick(attn_in, s)
    a_half[1] = pick(attn_in, 1 - s)
    cg = forward(yg, wg.at[rows_c, cols], cpeer)
    cu = forward(yu, wu.at[rows_c, cols], cpeer)
    kv_copy.wait_recv()
    kv_oth = kv[1]
    groups = H // KV
    bias3 = jnp.concatenate([bias] * groups, axis=0)

    def stack(value, g):
        return jnp.concatenate(
            [value[:, HD * j : HD * (j + 1)] for j in range(g * groups, (g + 1) * groups)], axis=0
        )

    def unstack(values):
        return [v[i * rows : (i + 1) * rows] for v in values for i in range(groups)]

    def keys(off, g):
        lo = off + HD * g
        return jnp.concatenate([kv_own[:, lo : lo + HD], kv_oth[:, lo : lo + HD]], axis=0)

    qs = [stack(qk, g) for g in range(KV)]
    ks = [keys(0, g) for g in range(KV)]
    vs = [keys(KV * HD, g) for g in range(KV)]
    outs = []
    for g in range(KV):
        sc = nt(qs[g], ks[g]) * HD ** (-0.5) + bias3
        top = jnp.max(sc, axis=-1, keepdims=True)
        lse = top + jnp.log(jnp.sum(jnp.exp(sc - top), axis=-1, keepdims=True))
        p = jnp.exp(sc - lse)
        probs[g] = p
        outs.append(nn(p.astype(BF16), vs[g]).astype(BF16))
    attended = jnp.concatenate(unstack(outs), axis=1)
    w_o = w5[1]
    middle = hidden + nn(attended, w_o)
    rr2 = lax.rsqrt(jnp.mean(middle * middle, axis=-1, keepdims=True) + norm_eps)
    normed2 = middle * rr2
    bb[0:rows] = (normed2 * ffn_g).astype(BF16)
    b_copy = remote(bb.at[pl.ds(0, rows)], bb.at[pl.ds(rows, rows)], xpeer)
    t_half[0] = pick(attended, s)
    t_half[1] = pick(attended, 1 - s)
    a_copy = remote(a_half.at[1], a_half.at[2], xpeer)
    for c in local[6:]:
        c.wait()
    cot_copy.wait_recv()
    grad_all = jnp.concatenate([cot_ref[...], cot[...]], axis=0)
    d_mix = nn(grad_all, down_ref[...])
    cg.wait_recv()
    cu.wait_recv()
    b_copy.wait_recv()
    ball = bb[...]
    gt = nn(ball, wg[...])
    up = nn(ball, wu[...])
    sig = jax.nn.sigmoid(gt)
    silu = gt * sig
    mix = (silu * up).astype(BF16)
    d_up = (d_mix * silu).astype(BF16)
    d_gt = (d_mix * up * sig * (1.0 + gt * (1.0 - sig))).astype(BF16)
    db = nt(d_gt, wg[...]) + nt(d_up, wu[...])
    dbo[...] = db[rows:].astype(BF16)
    db_copy = remote(dbo, dbi, xpeer)
    part = nt(mix, down_ref[...])
    part_out[...] = part[rows:].astype(BF16)
    part_copy = remote(part_out, part_in, xpeer)
    t_copy = remote(t_half.at[1], t_half.at[2], xpeer)

    gs, r1, r2, r3 = (g2, g1, g3), (r1b, r1a, r1c), (r2b, r2a, r2c), (r3b, r3a, r3c)
    fs, res = (f2, f1, f3), (o2_ref, o1_ref, o3_ref)
    state = [None] * 3

    def rs_core(p):
        state[p] = remote(gs[p].at[pl.ds((1 - core) * 8, 8)], r1[p], cpeer)

    def rs_y(p):
        state[p].wait_recv()

        @pl.loop(0, 8)
        def _(k):
            r1[p][k] = (r1[p][k].astype(F32) + gs[p][core * 8 + k].astype(F32)).astype(BF16)

        state[p] = remote(r1[p].at[pl.ds((1 - y) * 4, 4)], r2[p], ypeer)

    def rs_z(p):
        state[p].wait_recv()

        @pl.loop(0, 4)
        def _(k):
            r2[p][k] = (r2[p][k].astype(F32) + r1[p][y * 4 + k].astype(F32)).astype(BF16)

        state[p] = [
            remote(r2[p].at[(z + d) % 4], r3[p].at[d - 1], zpeers[d - 1]) for d in (1, 2, 3)
        ]

    def ag_z(p):
        for c in state[p]:
            c.wait_recv()
        total = r2[p][z].astype(F32)
        for d in range(3):
            total = total + r3[p][d].astype(F32)
        slot = core
        if p == 1:
            fs[p][0] = total.astype(BF16)
            i = counter[0]
            counter[0] += 1
            swap = pltpu.make_async_remote_copy(
                src_ref=fs[p].at[0], dst_ref=fs[p].at[1], send_sem=send_sem.at[i],
                recv_sem=recv_sem.at[i], device_id=xpeer, device_id_type=MESH,
            )

            @pl.when(core == 1)
            def _():
                swap.start()
                swap.wait()
                fs[p][0] = fs[p][1]

            slot = jnp.where(s == 0, core, 1 - core)
            res[p][slot * 8 + y * 4 + z] = fs[p][0]
        else:
            fs[p][0] = total.astype(BF16)
            res[p][slot * 8 + y * 4 + z] = fs[p][0]
        place = slot * 8 + y * 4 + z
        state[p] = [
            remote(fs[p].at[0], res[p].at[place], zpeers[d - 1]) for d in (1, 2, 3)
        ]
        return slot

    slots = [None] * 3

    def ag_y(p):
        for c in state[p]:
            c.wait_recv()
        block = res[p].at[pl.ds(slots[p] * 8 + y * 4, 4)]
        state[p] = remote(block, block, ypeer)

    def ag_core(p):
        state[p].wait_recv()
        block = res[p].at[pl.ds(slots[p] * 8, 8)]
        state[p] = remote(block, block, cpeer)

    g2[...] = tn(mix, grad_all).astype(BF16).reshape(g2.shape)
    rs_core(0)
    for half_t, dd in enumerate((d_gt, d_up)):
        gw = tn(ball, dd).astype(BF16)
        for h in range(2):
            for yy in range(2):
                for zz in range(2):
                    k = jnp.where(s == h, 0, 8) + yy * 4 + half_t * 2 + zz
                    lo = h * half + yy * hr
                    g1[k] = gw[lo : lo + hr, zz * 384 : (zz + 1) * 384]
    rs_core(1)
    db_copy.wait_recv()
    db = db[:rows] + dbi[...].astype(F32)
    gain2 = jnp.sum(db * normed2, axis=0, keepdims=True)
    e = db * ffn_g
    dm1 = cot_ref[...].astype(F32) + rr2 * (
        e - normed2 * jnp.mean(e * normed2, axis=-1, keepdims=True)
    )
    dm1b = dm1.astype(BF16)
    dm_x[0] = dm1b
    dm_copy = remote(dm_x.at[0], dm_x.at[1], xpeer)
    d_att = nt(dm1b, w_o).astype(BF16)
    rs_y(0)
    part_copy.wait_recv()
    out_ref[...] = middle + part[:rows] + part_in[...].astype(F32)

    dqs, dks, dvs = [], [], []
    for g in range(KV):
        do_g = stack(d_att, g)
        p = probs[g]
        dvs.append(tn(p.astype(BF16), do_g))
        delta = jnp.sum(do_g.astype(F32) * outs[g].astype(F32), axis=-1, keepdims=True)
        ds = (p * (nt(do_g, vs[g]) - delta) * HD ** (-0.5)).astype(BF16)
        dqs.append(nn(ds, ks[g]))
        dks.append(tn(ds, qs[g]))
        if g == 0:
            rs_y(1)
    dkv = jnp.concatenate(dks + dvs, axis=1)
    dkv_out[...] = dkv[rows:].astype(BF16)
    dkv_copy = remote(dkv_out, dkv_in, xpeer)
    rs_z(0)
    dkv_copy.wait_recv()
    dkv = dkv[:rows] + dkv_in[...].astype(F32)
    dqk = jnp.concatenate(unstack(dqs) + [dkv[:, : KV * HD]], axis=1)
    dqk = (dqk * cos_t - swap_halves(dqk) * sin_t).astype(BF16)
    dvb = dkv[:, KV * HD :].astype(BF16)
    dqk_x[0] = dqk
    dv_x[0] = dvb
    dqk_copy = remote(dqk_x.at[0], dqk_x.at[1], xpeer)
    dv_copy = remote(dv_x.at[0], dv_x.at[1], xpeer)
    da = nt(dqk[:, :576], w5[0]) + nt(dqk[:, 576:], w1[0]) + nt(dvb, w1[1])
    gain1 = jnp.sum(da * normed, axis=0, keepdims=True)
    gg_out[...] = jnp.concatenate([gain1, gain2, jnp.zeros((6, gain1.shape[1]), F32)], axis=0)
    gg_copy = remote(gg_out, gg_in, xpeer)
    rs_z(1)
    f = da * attn_g
    gin_ref[...] = dm1 + rr * (f - normed * jnp.mean(f * normed, axis=-1, keepdims=True))
    slots[0] = ag_z(0)
    for c in (a_copy, t_copy, dm_copy, dqk_copy, dv_copy):
        c.wait_recv()
    a_all = jnp.concatenate([a_half[0], a_half[2]], axis=0)
    t_all = jnp.concatenate([t_half[0], t_half[2]], axis=0)
    gw_o = tn(t_all, jnp.concatenate([dm_x[0], dm_x[1]], axis=0)).astype(BF16)
    gw_qk = tn(a_all, jnp.concatenate([dqk_x[0], dqk_x[1]], axis=0)).astype(BF16)
    gw_v = tn(a_all, jnp.concatenate([dv_x[0], dv_x[1]], axis=0)).astype(BF16)
    columns = [
        gw_qk[:, :384], gw_qk[:, 384:], gw_o[:, :384],
        jnp.concatenate([gw_o[:, 384:], gw_v], axis=1),
    ]
    gg_copy.wait_recv()
    gg = pick(gg_out[...] + gg_in[...], s)
    gg = jnp.concatenate([gg, jnp.zeros((8, 384 - dm), F32)], axis=1)
    row32 = lax.broadcasted_iota(jnp.int32, (32, 384), 0)
    for cc in range(4):
        for r in range(3):
            g3[r * 4 + cc] = columns[cc][r * 80 : (r + 1) * 80]
        g3[12 + cc, 0:48] = columns[cc][240:288]
        if cc < 2:
            tail = jnp.where(row32 == 0, jnp.broadcast_to(gg[cc : cc + 1], (32, 384)), 0.0)
        else:
            tail = jnp.zeros((32, 384), F32)
        g3[12 + cc, 48:80] = tail.astype(BF16)
    rs_core(2)
    rs_y(2)
    slots[1] = ag_z(1)
    rs_z(2)
    ag_y(0)
    slots[2] = ag_z(2)
    ag_y(1)
    ag_core(0)
    ag_y(2)
    ag_core(1)
    ag_core(2)
    for st in state:
        st.wait_recv()
    for c in started:
        c.wait_send()


def unpack_kernel(
    b_hbm, i_hbm, o1_hbm, o2_hbm, o3_hbm,
    block_ref, gin_ref, ag_ref, q_ref, k_ref, v_ref, o_ref, fg_ref, gate_ref, up_ref, down_ref,
    b_ref, i_ref, o1_ref, o2_ref, o3_ref, sem,
):
    pairs = (
        (b_hbm, b_ref), (i_hbm, i_ref), (o1_hbm, o1_ref), (o2_hbm, o2_ref), (o3_hbm, o3_ref),
    )
    copies = [pltpu.make_async_copy(src, dst, sem.at[i]) for i, (src, dst) in enumerate(pairs)]
    for c in copies:
        c.start()
    copies[0].wait()
    block_ref[...] = b_ref[...].T
    copies[1].wait()
    gin_ref[...] = i_ref[...].T
    copies[2].wait()
    half = ag_ref.shape[1]
    ffh = gate_ref.shape[2] // 2
    for f in range(2):
        for yy in range(2):
            for t, ref in enumerate((gate_ref, up_ref)):
                for zz in range(2):
                    lo = f * ffh + zz * 384
                    ref[0, yy * 144 : (yy + 1) * 144, lo : lo + 384] = o1_ref[
                        f * 8 + yy * 4 + t * 2 + zz
                    ].astype(F32)
    copies[3].wait()
    down_ref[0] = o2_ref[...].reshape(down_ref.shape[1:]).astype(F32)
    copies[4].wait()
    for r in range(4):
        lo = r * 80
        n = 80 if r < 3 else 48
        rows = slice(lo, lo + n)
        q_ref[0, rows, :384] = o3_ref[r * 4, :n].astype(F32)
        mid = o3_ref[r * 4 + 1, :n].astype(F32)
        q_ref[0, rows, 384:] = mid[:, :192]
        k_ref[0, rows] = mid[:, 192:]
        o_ref[0, rows, :384] = o3_ref[r * 4 + 2, :n].astype(F32)
        last = o3_ref[r * 4 + 3, :n].astype(F32)
        o_ref[0, rows, 384:] = last[:, :192]
        v_ref[0, rows] = last[:, 192:]
    ag_ref[...] = o3_ref[12, 48:64].astype(F32)[0:1, :half]
    fg_ref[...] = o3_ref[13, 48:64].astype(F32)[0:1, :half]


def fused_body(
    tokens, block_order, attn_gain, q_weight, k_weight, v_weight, o_weight, ffn_gain,
    gate_weight, up_weight, down_weight, cotangent,
):
    rows, width = tokens.shape
    half = attn_gain.shape[1]
    ff = gate_weight.shape[2]
    vm = pl.BlockSpec(memory_space=pltpu.VMEM)
    hbm = pl.BlockSpec(memory_space=pl.ANY)
    shapes = [(144, 384), (48, width), (80, 384)]

    def buf(*shape, dtype=BF16):
        return pltpu.VMEM(shape, dtype)

    scratch = [
        buf(width, rows), buf(width, rows), buf(rows, width), buf(width, ff // 2),
        buf(2, width, width),
        buf(2, width, KV * HD), buf(width, ff // 2), buf(width, ff // 2),
        buf(8, width, dtype=F32), buf(8, width, dtype=F32),
        buf(rows, width), buf(2, rows, 384), buf(2 * rows, width), buf(rows, width),
        buf(rows, width), buf(rows, width), buf(rows, width),
        buf(KV, 3 * rows, 2 * rows, dtype=F32), buf(3, rows, half), buf(3, rows, half),
        buf(2, rows, width), buf(rows, 384), buf(rows, 384), buf(2, rows, 768),
        buf(2, rows, 192), buf(8, width, dtype=F32), buf(8, width, dtype=F32),
    ]
    for count in (16, 8, 4, 3, 2):
        scratch += [buf(count, *sh) for sh in shapes]
    scratch += [
        pltpu.SemaphoreType.DMA((64,)), pltpu.SemaphoreType.DMA((64,)),
        pltpu.SemaphoreType.DMA((9,)),
    ]
    block_out, input_grad, o1, o2, o3 = pl.pallas_call(
        fused_kernel,
        out_shape=(
            jax.ShapeDtypeStruct((rows, width), F32),
            jax.ShapeDtypeStruct((rows, width), F32),
            *[jax.ShapeDtypeStruct((16, *sh), BF16) for sh in shapes],
        ),
        in_specs=[
            hbm, pl.BlockSpec(memory_space=pltpu.SMEM), vm, *[hbm] * 4, vm, *[hbm] * 4,
        ],
        out_specs=[vm] * 5,
        scratch_shapes=scratch,
        compiler_params=pltpu.CompilerParams(
            collective_id=0, has_side_effects=True, vmem_limit_bytes=56 * 1024 * 1024
        ),
    )(
        tokens.T, block_order, attn_gain, q_weight, k_weight, v_weight, o_weight, ffn_gain,
        gate_weight, up_weight, down_weight[0].T, cotangent.T,
    )
    out_shapes = [
        (width, rows), (width, rows), (1, half), (1, half, width), (1, half, KV * HD),
        (1, half, KV * HD), (1, half, width), (1, half), (1, half, ff), (1, half, ff),
        (1, ff // 2, width),
    ]
    out = pl.pallas_call(
        unpack_kernel,
        out_shape=tuple(jax.ShapeDtypeStruct(shape, F32) for shape in out_shapes),
        in_specs=[hbm] * 5,
        out_specs=(vm,) * 11,
        scratch_shapes=[
            buf(rows, width, dtype=F32), buf(rows, width, dtype=F32),
            *[buf(16, *sh) for sh in shapes], pltpu.SemaphoreType.DMA((5,)),
        ],
        compiler_params=pltpu.CompilerParams(vmem_limit_bytes=40 * 1024 * 1024),
    )(block_out, input_grad, o1, o2, o3)
    return (out[0].T, out[1].T, *out[2:])


def solution(mesh):
    placed = (
        P(("rep", "shard"), None),
        P("rep", None),
        P(None, "shard"),
        P(None, "shard", None),
        P(None, "shard", None),
        P(None, "shard", None),
        P(None, "shard", None),
        P(None, "shard"),
        P(None, "shard", None),
        P(None, "shard", None),
        P(None, "shard", None),
        P(("rep", "shard"), None),
    )
    fused = mesh.shape["shard"] == 2 and mesh.shape["rep"] == 16
    return jax.shard_map(
        fused_body if fused else body,
        mesh=mesh,
        in_specs=placed,
        out_specs=(
            P(("rep", "shard"), None),
            P(("rep", "shard"), None),
            P(None, "shard"),
            P(None, "shard", None),
            P(None, "shard", None),
            P(None, "shard", None),
            P(None, "shard", None),
            P(None, "shard"),
            P(None, "shard", None),
            P(None, "shard", None),
            P(None, "shard", None),
        ),
        check_vma=False,
    )
```

```python
import math

import jax
import jax.numpy as jnp
from jax import lax
from jax.experimental import pallas as pl
from jax.experimental.pallas import tpu as pltpu
from jax.sharding import PartitionSpec as P

H = 9
KV = 3
HD = 64
LAYERS = 1


rope_base = 100000.0
norm_eps = 1e-05


def rope_tables(positions, head_dim):
    half_dim = head_dim // 2
    frequency = jnp.exp(
        jnp.arange(half_dim, dtype=jnp.float32) * (-2.0 * math.log(rope_base) / head_dim)
    )
    angles = positions.astype(jnp.float32)[:, None] * frequency[None, :]
    return (jnp.cos(angles)[:, None, :], jnp.sin(angles)[:, None, :])


def rotate(tensor, cos_table, sin_table):
    half_dim = tensor.shape[-1] // 2
    first_half = tensor[..., :half_dim]
    second_half = tensor[..., half_dim:]
    return jnp.concatenate(
        [
            first_half * cos_table - second_half * sin_table,
            second_half * cos_table + first_half * sin_table,
        ],
        axis=-1,
    )


def rotate_back(tensor, cos_table, sin_table):
    half_dim = tensor.shape[-1] // 2
    first_half = tensor[..., :half_dim]
    second_half = tensor[..., half_dim:]
    return jnp.concatenate(
        [
            first_half * cos_table + second_half * sin_table,
            second_half * cos_table - first_half * sin_table,
        ],
        axis=-1,
    )


def rms_scale(hidden):
    factor = lax.rsqrt(jnp.mean(hidden * hidden, axis=-1, keepdims=True) + norm_eps)
    return (hidden * factor, factor)


def rms_back(grad_in, normed, factor, gain_row):
    scaled = grad_in * gain_row.astype(jnp.float32)
    return factor * (scaled - normed * jnp.mean(scaled * normed, axis=-1, keepdims=True))


def transposed_product(left, right):
    return jnp.einsum("tk,tn->kn", left, right, preferred_element_type=jnp.float32)


def gather_forward(params, layer_index):
    return (
        lax.all_gather(params[0][layer_index], "shard", axis=0, tiled=True),
        lax.all_gather(params[1][layer_index], "shard", axis=0, tiled=True),
        lax.all_gather(params[2][layer_index], "shard", axis=0, tiled=True),
        lax.all_gather(params[3][layer_index], "shard", axis=0, tiled=True),
        lax.all_gather(params[4][layer_index], "shard", axis=0, tiled=True),
        lax.all_gather(params[5][layer_index], "shard", axis=0, tiled=True),
        lax.all_gather(params[6][layer_index], "shard", axis=0, tiled=True),
        lax.all_gather(params[7][layer_index], "shard", axis=0, tiled=True),
        lax.all_gather(params[8][layer_index], "shard", axis=0, tiled=True),
    )


def gather_backward(params, layer_index):
    return (
        lax.all_gather(params[0][layer_index], "shard", axis=0, tiled=True),
        lax.all_gather(params[1][layer_index], "shard", axis=0, tiled=True),
        lax.all_gather(params[2][layer_index], "shard", axis=0, tiled=True),
        lax.all_gather(params[3][layer_index], "shard", axis=0, tiled=True),
        lax.all_gather(params[4][layer_index], "shard", axis=0, tiled=True),
        lax.all_gather(params[5][layer_index], "shard", axis=0, tiled=True),
        lax.all_gather(params[6][layer_index], "shard", axis=0, tiled=True),
        lax.all_gather(params[7][layer_index], "shard", axis=0, tiled=True),
        lax.all_gather(params[8][layer_index], "shard", axis=0, tiled=True),
    )


def visible_scores(query_grouped, all_keys, q_positions, key_positions):
    scores = jnp.einsum(
        "sgmd,tgd->gmst", query_grouped, all_keys, preferred_element_type=jnp.float32
    ) * HD ** (-0.5)
    allowed = key_positions[None, :] <= q_positions[:, None]
    return (jnp.where(allowed, scores, -1e30), allowed)


def layer_forward(hidden, gathered, q_positions, key_positions, cos_table, sin_table):
    attn_g, q_w, k_w, v_w, o_w, ffn_g, gate_w, up_w, down_w = gathered
    row_count = hidden.shape[0]
    head_groups = H // KV
    normed, factor = rms_scale(hidden)
    attn_in = (normed * attn_g.astype(jnp.float32)).astype(jnp.bfloat16)
    query_rows = rotate(
        jnp.dot(attn_in, q_w, preferred_element_type=jnp.float32).reshape(row_count, H, HD),
        cos_table,
        sin_table,
    ).astype(jnp.bfloat16)
    key_rows = rotate(
        jnp.dot(attn_in, k_w, preferred_element_type=jnp.float32).reshape(row_count, KV, HD),
        cos_table,
        sin_table,
    ).astype(jnp.bfloat16)
    value_rows = jnp.dot(attn_in, v_w, preferred_element_type=jnp.float32).astype(jnp.bfloat16)
    all_keys, all_values = (
        lax.all_gather(key_rows.reshape(row_count, KV * HD), "shard", axis=0, tiled=True),
        lax.all_gather(value_rows, "shard", axis=0, tiled=True),
    )
    all_keys = all_keys.reshape(-1, KV, HD)
    all_values = all_values.reshape(-1, KV, HD)
    query_grouped = query_rows.reshape(row_count, KV, head_groups, HD)
    scores, allowed = visible_scores(query_grouped, all_keys, q_positions, key_positions)
    row_max = jnp.max(scores, axis=-1, keepdims=True)
    row_total = jnp.sum(jnp.exp(scores - row_max), axis=-1, keepdims=True)
    log_total = (row_max + jnp.log(row_total))[..., 0]
    probs_bf = jnp.where(allowed, jnp.exp(scores - log_total[..., None]), 0.0).astype(jnp.bfloat16)
    attended = (
        jnp.einsum("gmst,tgd->sgmd", probs_bf, all_values, preferred_element_type=jnp.float32)
        .astype(jnp.bfloat16)
        .reshape(row_count, H * HD)
    )
    middle = hidden + jnp.dot(attended, o_w, preferred_element_type=jnp.float32)
    normed_two, factor_two = rms_scale(middle)
    ffn_in = (normed_two * ffn_g.astype(jnp.float32)).astype(jnp.bfloat16)
    gate_pre = jnp.dot(ffn_in, gate_w, preferred_element_type=jnp.float32)
    up_pre = jnp.dot(ffn_in, up_w, preferred_element_type=jnp.float32)
    mixed = (jax.nn.silu(gate_pre) * up_pre).astype(jnp.bfloat16)
    output = middle + jnp.dot(mixed, down_w, preferred_element_type=jnp.float32)
    saved = (
        normed,
        factor,
        attn_in,
        query_grouped,
        all_keys,
        all_values,
        log_total,
        attended,
        normed_two,
        factor_two,
        ffn_in,
        gate_pre,
        up_pre,
        mixed,
    )
    return (output, saved)


def layer_backward(gradient, saved, gathered, q_positions, key_positions, cos_table, sin_table):
    attn_g, q_w, k_w, v_w, o_w, ffn_g, gate_w, up_w, down_w = gathered
    (
        normed,
        factor,
        attn_in,
        query_grouped,
        all_keys,
        all_values,
        log_total,
        attended,
        normed_two,
        factor_two,
        ffn_in,
        gate_pre,
        up_pre,
        mixed,
    ) = saved
    row_count = gradient.shape[0]
    head_groups = H // KV
    grad_bf = gradient.astype(jnp.bfloat16)
    g_down = transposed_product(mixed, grad_bf)
    g_mixed = jnp.einsum("tn,kn->tk", grad_bf, down_w, preferred_element_type=jnp.float32)
    sigmoid_gate = jax.nn.sigmoid(gate_pre)
    g_up = (g_mixed * gate_pre * sigmoid_gate).astype(jnp.bfloat16)
    g_gate = (g_mixed * up_pre * sigmoid_gate * (1.0 + gate_pre * (1.0 - sigmoid_gate))).astype(
        jnp.bfloat16
    )
    g_gate_w = transposed_product(ffn_in, g_gate)
    g_up_w = transposed_product(ffn_in, g_up)
    g_ffn_in = jnp.einsum(
        "tn,kn->tk", g_gate, gate_w, preferred_element_type=jnp.float32
    ) + jnp.einsum("tn,kn->tk", g_up, up_w, preferred_element_type=jnp.float32)
    g_ffn_gain = jnp.sum(g_ffn_in * normed_two, axis=0)
    g_middle = gradient + rms_back(g_ffn_in, normed_two, factor_two, ffn_g)
    middle_bf = g_middle.astype(jnp.bfloat16)
    g_o_w = transposed_product(attended, middle_bf)
    g_attended = (
        jnp.einsum("tn,kn->tk", middle_bf, o_w, preferred_element_type=jnp.float32)
        .astype(jnp.bfloat16)
        .reshape(row_count, KV, head_groups, HD)
    )
    scores, allowed = visible_scores(query_grouped, all_keys, q_positions, key_positions)
    probs = jnp.where(allowed, jnp.exp(scores - log_total[..., None]), 0.0)
    probs_bf = probs.astype(jnp.bfloat16)
    value_terms = jnp.einsum(
        "gmst,sgmd->tgd", probs_bf, g_attended, preferred_element_type=jnp.float32
    )
    g_probs = jnp.einsum(
        "sgmd,tgd->gmst", g_attended, all_values, preferred_element_type=jnp.float32
    )
    delta = jnp.einsum(
        "sgmd,sgmd->gms",
        g_attended,
        attended.reshape(row_count, KV, head_groups, HD),
        preferred_element_type=jnp.float32,
    )
    g_scores = (probs * (g_probs - delta[..., None]) * HD ** (-0.5)).astype(jnp.bfloat16)
    g_query = jnp.einsum("gmst,tgd->sgmd", g_scores, all_keys, preferred_element_type=jnp.float32)
    key_terms = jnp.einsum(
        "gmst,sgmd->tgd", g_scores, query_grouped, preferred_element_type=jnp.float32
    )
    seq_rows = key_terms.shape[0]
    key_sum, value_sum = (
        lax.psum_scatter(
            key_terms.reshape(seq_rows, KV * HD), "shard", scatter_dimension=0, tiled=True
        ),
        lax.psum_scatter(
            value_terms.reshape(seq_rows, KV * HD), "shard", scatter_dimension=0, tiled=True
        ),
    )
    g_query_bf = (
        rotate_back(g_query.reshape(row_count, H, HD), cos_table, sin_table)
        .reshape(row_count, H * HD)
        .astype(jnp.bfloat16)
    )
    g_key_bf = (
        rotate_back(key_sum.reshape(row_count, KV, HD), cos_table, sin_table)
        .reshape(row_count, KV * HD)
        .astype(jnp.bfloat16)
    )
    g_value_bf = value_sum.astype(jnp.bfloat16)
    g_q_w = transposed_product(attn_in, g_query_bf)
    g_k_w = transposed_product(attn_in, g_key_bf)
    g_v_w = transposed_product(attn_in, g_value_bf)
    g_attn_in = (
        jnp.einsum("tn,kn->tk", g_query_bf, q_w, preferred_element_type=jnp.float32)
        + jnp.einsum("tn,kn->tk", g_key_bf, k_w, preferred_element_type=jnp.float32)
        + jnp.einsum("tn,kn->tk", g_value_bf, v_w, preferred_element_type=jnp.float32)
    )
    g_attn_gain = jnp.sum(g_attn_in * normed, axis=0)
    g_hidden = g_middle + rms_back(g_attn_in, normed, factor, attn_g)
    terms = (g_attn_gain, g_q_w, g_k_w, g_v_w, g_o_w, g_ffn_gain, g_gate_w, g_up_w, g_down)
    return (g_hidden, terms)


def share_terms(terms):
    return (
        lax.psum_scatter(terms[0], "shard", scatter_dimension=0, tiled=True),
        lax.psum_scatter(terms[1], "shard", scatter_dimension=0, tiled=True),
        lax.psum_scatter(terms[2], "shard", scatter_dimension=0, tiled=True),
        lax.psum_scatter(terms[3], "shard", scatter_dimension=0, tiled=True),
        lax.psum_scatter(terms[4], "shard", scatter_dimension=0, tiled=True),
        lax.psum_scatter(terms[5], "shard", scatter_dimension=0, tiled=True),
        lax.psum_scatter(terms[6], "shard", scatter_dimension=0, tiled=True),
        lax.psum_scatter(terms[7], "shard", scatter_dimension=0, tiled=True),
        lax.psum_scatter(terms[8], "shard", scatter_dimension=0, tiled=True),
    )


def replica_sum(shares):
    return lax.psum(
        (
            shares[0],
            shares[1],
            shares[2],
            shares[3],
            shares[4],
            shares[5],
            shares[6],
            shares[7],
            shares[8],
        ),
        "rep",
    )


def body(
    tokens,
    block_order,
    attn_gain,
    q_weight,
    k_weight,
    v_weight,
    o_weight,
    ffn_gain,
    gate_weight,
    up_weight,
    down_weight,
    cotangent,
):
    row_count = tokens.shape[0]
    order_row = block_order[0]
    own_block = lax.dynamic_index_in_dim(order_row, lax.axis_index("shard"), 0, keepdims=False)
    local_index = jnp.arange(row_count, dtype=jnp.int32)
    q_positions = own_block * row_count + local_index
    key_positions = (order_row[:, None] * row_count + local_index[None, :]).reshape(-1)
    cos_table, sin_table = rope_tables(q_positions, HD)
    params = (
        attn_gain,
        q_weight,
        k_weight,
        v_weight,
        o_weight,
        ffn_gain,
        gate_weight,
        up_weight,
        down_weight,
    )
    hidden = tokens.astype(jnp.float32)
    kept_weights = []
    layer_index = 0
    gathered = gather_forward(params, layer_index)
    hidden, saved = layer_forward(
        hidden, gathered, q_positions, key_positions, cos_table, sin_table
    )
    saved_list = [saved]
    kept_weights.append(gathered)
    gradient = cotangent.astype(jnp.float32)
    reduced = [None] * LAYERS
    for layer_index in reversed(range(LAYERS)):
        gathered = gather_backward(params, layer_index)
        gradient, terms = layer_backward(
            gradient,
            saved_list[layer_index],
            gathered,
            q_positions,
            key_positions,
            cos_table,
            sin_table,
        )
        shares = replica_sum(share_terms(terms))
        reduced[layer_index] = shares
    stacked = tuple((jnp.stack([reduced[0][member]]) for member in range(9)))
    return (
        hidden,
        gradient,
        stacked[0],
        stacked[1],
        stacked[2],
        stacked[3],
        stacked[4],
        stacked[5],
        stacked[6],
        stacked[7],
        stacked[8],
    )


F32 = jnp.float32
BF16 = jnp.bfloat16
MESH = pl.DeviceIdType.MESH


def nn(left, right):
    return lax.dot_general(left, right, (((1,), (0,)), ((), ())), preferred_element_type=F32)


def nt(left, right):
    return lax.dot_general(left, right, (((1,), (1,)), ((), ())), preferred_element_type=F32)


def tn(left, right):
    return lax.dot_general(left, right, (((0,), (0,)), ((), ())), preferred_element_type=F32)


def swap_halves(x):
    width = x.shape[-1]
    lane = lax.broadcasted_iota(jnp.int32, x.shape, 1)
    return jnp.where(
        lane % HD < HD // 2, pltpu.roll(x, width - HD // 2, 1), pltpu.roll(x, HD // 2, 1)
    )


def fused_kernel(
    tok_hbm, order_ref, again_ref, q_hbm, k_hbm, v_hbm, o_hbm, fgain_ref, gate_hbm, up_hbm, down_hbm,
    cot_hbm,
    out_ref, gin_ref, o1_ref, o2_ref, o3_ref,
    tok_t, cot_t, cot_ref, down_ref, w5, w1, wg, wu, gain_ref, gain_in, cot, kv, bb, part_out, part_in, dbo, dbi, probs, a_half, t_half, dm_x,
    dkv_out, dkv_in, dqk_x, dv_x, gg_out, gg_in, g1, g2, g3, r1a, r1b, r1c, r2a, r2b, r2c,
    r3a, r3b, r3c, f1, f2, f3, send_sem, recv_sem, local_sem,
):
    rows = tok_t.shape[1]
    rep = lax.axis_index("rep")
    s = lax.axis_index("shard")
    core = rep % 2
    y = (rep // 2) % 2
    z = rep // 4
    xpeer = (rep, 1 - s)
    cpeer = (rep + 1 - 2 * core, s)
    ypeer = (rep + 2 - 4 * y, s)

    def zdev(z2):
        return (z2 * 4 + y * 2 + core, s)

    zpeers = [zdev((z + d) % 4) for d in (1, 2, 3)]
    counter = [0]
    started = []

    def remote(src, dst, device):
        i = counter[0]
        counter[0] += 1
        c = pltpu.make_async_remote_copy(
            src_ref=src, dst_ref=dst, send_sem=send_sem.at[i], recv_sem=recv_sem.at[i],
            device_id=device, device_id_type=MESH,
        )
        c.start()
        started.append(c)
        return c

    gate_ref, up_ref = gate_hbm.at[0], up_hbm.at[0]
    half = gate_ref.shape[0]
    ffh = wg.shape[1]
    mine = pl.multiple_of(s * half, 16)
    theirs = pl.multiple_of((1 - s) * half, 16)
    ffcols = pl.ds(pl.multiple_of(s * ffh, 128), ffh)
    own_rows = pl.ds(mine, half)
    pairs = [
        (q_hbm.at[0], w5.at[0, own_rows]), (o_hbm.at[0], w5.at[1, own_rows]),
        (k_hbm.at[0], w1.at[0, own_rows]), (v_hbm.at[0], w1.at[1, own_rows]),
        (tok_hbm, tok_t), (cot_hbm, cot_t), (gate_ref.at[:, ffcols], wg.at[own_rows]),
        (up_ref.at[:, ffcols], wu.at[own_rows]), (down_hbm, down_ref),
    ]
    local = [
        pltpu.make_async_copy(src, dst, local_sem.at[i]) for i, (src, dst) in enumerate(pairs)
    ]
    for c in local:
        c.start()

    lane = lax.broadcasted_iota(jnp.int32, (rows, 128), 1)
    sub = lax.broadcasted_iota(jnp.int32, (rows, 128), 0)
    own, other = order_ref[0, s], order_ref[0, 1 - s]
    position = own * rows + sub
    frequency = jnp.exp((lane % (HD // 2)).astype(F32) * (-2.0 * math.log(rope_base) / HD))
    angle = position.astype(F32) * frequency
    cos_t = jnp.cos(angle)
    sin_t = jnp.sin(angle)
    sin_t = jnp.where(lane % HD < HD // 2, -sin_t, sin_t)
    cos_t = jnp.concatenate([cos_t] * 6, axis=1)
    sin_t = jnp.concatenate([sin_t] * 6, axis=1)
    bias = jnp.concatenate(
        [
            jnp.where(start * rows + lane <= position, 0.0, -1e30).astype(F32)
            for start in (own, other)
        ],
        axis=1,
    )
    both = jnp.concatenate([again_ref[...], fgain_ref[...]], axis=0).astype(F32)
    none = jnp.zeros_like(both)
    gain_ref[0:2] = jnp.where(
        s == 0,
        jnp.concatenate([both, none], axis=1),
        jnp.concatenate([none, both], axis=1),
    )
    gain_ref[2:8] = jnp.zeros((6, 2 * half), F32)

    local[5].wait()
    cot_ref[...] = cot_t[...].astype(F32).T.astype(BF16)
    barrier = pltpu.get_barrier_semaphore()
    for peer in [xpeer, cpeer, ypeer] + zpeers:
        pl.semaphore_signal(barrier, inc=1, device_id=peer, device_id_type=MESH)
    pl.semaphore_wait(barrier, 6)

    gain_copy = remote(gain_ref, gain_in, xpeer)
    for c in local[:4]:
        c.wait()
    hr = half // 2
    rows_x = pl.ds(pl.multiple_of(s * half + y * hr, 16), hr)
    rows_y = pl.ds(pl.multiple_of(theirs + y * hr, 16), hr)
    part_x = pl.ds(pl.multiple_of(y * hr, 16), hr)
    hc = ffh // 2
    cols = pl.ds(pl.multiple_of(core * hc, 128), hc)
    cols_x = pl.ds(pl.multiple_of((1 - s) * ffh + core * hc, 128), hc)

    def send(block, device):
        return remote(block, block, device)

    x5 = send(w5.at[core, rows_x], xpeer)
    x1 = send(w1.at[core, rows_x], xpeer)
    xg = remote(gate_ref.at[part_x, cols_x], wg.at[rows_x, cols], xpeer)
    xu = remote(up_ref.at[part_x, cols_x], wu.at[rows_x, cols], xpeer)
    cot_copy = remote(cot_ref, cot, xpeer)
    rows_c = pl.ds(theirs, half)

    def forward(copy, block, device):
        copy.wait_recv()
        return send(block, device)

    y5 = forward(x5, w5.at[core, rows_y], ypeer)
    y1 = forward(x1, w1.at[core, rows_y], ypeer)
    local[4].wait()
    hidden = tok_t[...].astype(F32).T
    rr = lax.rsqrt(jnp.mean(hidden * hidden, axis=-1, keepdims=True) + norm_eps)
    normed = hidden * rr
    gain_copy.wait_recv()
    gains = gain_ref[...] + gain_in[...]
    attn_g = gains[0:1, :]
    ffn_g = gains[1:2, :]
    attn_in = (normed * attn_g).astype(BF16)
    c5 = forward(y5, w5.at[core, rows_c], cpeer)
    c1 = forward(y1, w1.at[core, rows_c], cpeer)
    yg = forward(xg, wg.at[rows_y, cols], ypeer)
    yu = forward(xu, wu.at[rows_y, cols], ypeer)
    dm = attn_in.shape[1] // 2

    def pick(value, flag):
        return jnp.where(flag == 0, value[:, :dm], value[:, dm:])

    c5.wait_recv()
    c1.wait_recv()
    qk = jnp.concatenate([nn(attn_in, w5[0]), nn(attn_in, w1[0])], axis=1)
    qk = (qk * cos_t + swap_halves(qk) * sin_t).astype(BF16)
    v = nn(attn_in, w1[1]).astype(BF16)
    kv_own = jnp.concatenate([qk[:, 576:768], v], axis=1)
    kv[0] = kv_own
    kv_copy = remote(kv.at[0], kv.at[1], xpeer)
    a_half[0] = pick(attn_in, s)
    a_half[1] = pick(attn_in, 1 - s)
    cg = forward(yg, wg.at[rows_c, cols], cpeer)
    cu = forward(yu, wu.at[rows_c, cols], cpeer)
    kv_copy.wait_recv()
    kv_oth = kv[1]
    groups = H // KV
    bias3 = jnp.concatenate([bias] * groups, axis=0)

    def stack(value, g):
        return jnp.concatenate(
            [value[:, HD * j : HD * (j + 1)] for j in range(g * groups, (g + 1) * groups)], axis=0
        )

    def unstack(values):
        return [v[i * rows : (i + 1) * rows] for v in values for i in range(groups)]

    def keys(off, g):
        lo = off + HD * g
        return jnp.concatenate([kv_own[:, lo : lo + HD], kv_oth[:, lo : lo + HD]], axis=0)

    qs = [stack(qk, g) for g in range(KV)]
    ks = [keys(0, g) for g in range(KV)]
    vs = [keys(KV * HD, g) for g in range(KV)]
    outs = []
    for g in range(KV):
        sc = nt(qs[g], ks[g]) * HD ** (-0.5) + bias3
        top = jnp.max(sc, axis=-1, keepdims=True)
        lse = top + jnp.log(jnp.sum(jnp.exp(sc - top), axis=-1, keepdims=True))
        p = jnp.exp(sc - lse)
        probs[g] = p
        outs.append(nn(p.astype(BF16), vs[g]).astype(BF16))
    attended = jnp.concatenate(unstack(outs), axis=1)
    w_o = w5[1]
    middle = hidden + nn(attended, w_o)
    rr2 = lax.rsqrt(jnp.mean(middle * middle, axis=-1, keepdims=True) + norm_eps)
    normed2 = middle * rr2
    bb[0:rows] = (normed2 * ffn_g).astype(BF16)
    b_copy = remote(bb.at[pl.ds(0, rows)], bb.at[pl.ds(rows, rows)], xpeer)
    t_half[0] = pick(attended, s)
    t_half[1] = pick(attended, 1 - s)
    a_copy = remote(a_half.at[1], a_half.at[2], xpeer)
    for c in local[6:]:
        c.wait()
    cot_copy.wait_recv()
    grad_all = jnp.concatenate([cot_ref[...], cot[...]], axis=0)
    d_mix = nn(grad_all, down_ref[...])
    cg.wait_recv()
    cu.wait_recv()
    b_copy.wait_recv()
    ball = bb[...]
    gt = nn(ball, wg[...])
    up = nn(ball, wu[...])
    sig = jax.nn.sigmoid(gt)
    silu = gt * sig
    mix = (silu * up).astype(BF16)
    d_up = (d_mix * silu).astype(BF16)
    d_gt = (d_mix * up * sig * (1.0 + gt * (1.0 - sig))).astype(BF16)
    db = nt(d_gt, wg[...]) + nt(d_up, wu[...])
    dbo[...] = db[rows:].astype(BF16)
    db_copy = remote(dbo, dbi, xpeer)
    part = nt(mix, down_ref[...])
    part_out[...] = part[rows:].astype(BF16)
    part_copy = remote(part_out, part_in, xpeer)
    t_copy = remote(t_half.at[1], t_half.at[2], xpeer)

    gs, r1, r2, r3 = (g2, g1, g3), (r1b, r1a, r1c), (r2b, r2a, r2c), (r3b, r3a, r3c)
    fs, res = (f2, f1, f3), (o2_ref, o1_ref, o3_ref)
    state = [None] * 3

    def rs_core(p):
        state[p] = remote(gs[p].at[pl.ds((1 - core) * 8, 8)], r1[p], cpeer)

    def rs_y(p):
        state[p].wait_recv()

        @pl.loop(0, 8)
        def _(k):
            r1[p][k] = (r1[p][k].astype(F32) + gs[p][core * 8 + k].astype(F32)).astype(BF16)

        state[p] = remote(r1[p].at[pl.ds((1 - y) * 4, 4)], r2[p], ypeer)

    def rs_z(p):
        state[p].wait_recv()

        @pl.loop(0, 4)
        def _(k):
            r2[p][k] = (r2[p][k].astype(F32) + r1[p][y * 4 + k].astype(F32)).astype(BF16)

        state[p] = [
            remote(r2[p].at[(z + d) % 4], r3[p].at[d - 1], zpeers[d - 1]) for d in (1, 2, 3)
        ]

    def ag_z(p):
        for c in state[p]:
            c.wait_recv()
        total = r2[p][z].astype(F32)
        for d in range(3):
            total = total + r3[p][d].astype(F32)
        slot = core
        if p == 1:
            fs[p][0] = total.astype(BF16)
            i = counter[0]
            counter[0] += 1
            swap = pltpu.make_async_remote_copy(
                src_ref=fs[p].at[0], dst_ref=fs[p].at[1], send_sem=send_sem.at[i],
                recv_sem=recv_sem.at[i], device_id=xpeer, device_id_type=MESH,
            )

            @pl.when(core == 1)
            def _():
                swap.start()
                swap.wait()
                fs[p][0] = fs[p][1]

            slot = jnp.where(s == 0, core, 1 - core)
            res[p][slot * 8 + y * 4 + z] = fs[p][0]
        else:
            fs[p][0] = total.astype(BF16)
            res[p][slot * 8 + y * 4 + z] = fs[p][0]
        place = slot * 8 + y * 4 + z
        state[p] = [
            remote(fs[p].at[0], res[p].at[place], zpeers[d - 1]) for d in (1, 2, 3)
        ]
        return slot

    slots = [None] * 3

    def ag_y(p):
        for c in state[p]:
            c.wait_recv()
        block = res[p].at[pl.ds(slots[p] * 8 + y * 4, 4)]
        state[p] = remote(block, block, ypeer)

    def ag_core(p):
        state[p].wait_recv()
        block = res[p].at[pl.ds(slots[p] * 8, 8)]
        state[p] = remote(block, block, cpeer)

    g2[...] = tn(mix, grad_all).astype(BF16).reshape(g2.shape)
    rs_core(0)
    for half_t, dd in enumerate((d_gt, d_up)):
        gw = tn(ball, dd).astype(BF16)
        for h in range(2):
            for yy in range(2):
                for zz in range(2):
                    k = jnp.where(s == h, 0, 8) + yy * 4 + half_t * 2 + zz
                    lo = h * half + yy * hr
                    g1[k] = gw[lo : lo + hr, zz * 384 : (zz + 1) * 384]
    rs_core(1)
    db_copy.wait_recv()
    db = db[:rows] + dbi[...].astype(F32)
    gain2 = jnp.sum(db * normed2, axis=0, keepdims=True)
    e = db * ffn_g
    dm1 = cot_ref[...].astype(F32) + rr2 * (
        e - normed2 * jnp.mean(e * normed2, axis=-1, keepdims=True)
    )
    dm1b = dm1.astype(BF16)
    dm_x[0] = dm1b
    dm_copy = remote(dm_x.at[0], dm_x.at[1], xpeer)
    d_att = nt(dm1b, w_o).astype(BF16)
    rs_y(0)
    part_copy.wait_recv()
    out_ref[...] = middle + part[:rows] + part_in[...].astype(F32)

    dqs, dks, dvs = [], [], []
    for g in range(KV):
        do_g = stack(d_att, g)
        p = probs[g]
        dvs.append(tn(p.astype(BF16), do_g))
        delta = jnp.sum(do_g.astype(F32) * outs[g].astype(F32), axis=-1, keepdims=True)
        ds = (p * (nt(do_g, vs[g]) - delta) * HD ** (-0.5)).astype(BF16)
        dqs.append(nn(ds, ks[g]))
        dks.append(tn(ds, qs[g]))
        if g == 0:
            rs_y(1)
    dkv = jnp.concatenate(dks + dvs, axis=1)
    dkv_out[...] = dkv[rows:].astype(BF16)
    dkv_copy = remote(dkv_out, dkv_in, xpeer)
    rs_z(0)
    rs_z(1)
    dkv_copy.wait_recv()
    dkv = dkv[:rows] + dkv_in[...].astype(F32)
    dqk = jnp.concatenate(unstack(dqs) + [dkv[:, : KV * HD]], axis=1)
    dqk = (dqk * cos_t - swap_halves(dqk) * sin_t).astype(BF16)
    dvb = dkv[:, KV * HD :].astype(BF16)
    dqk_x[0] = dqk
    dv_x[0] = dvb
    dqk_copy = remote(dqk_x.at[0], dqk_x.at[1], xpeer)
    dv_copy = remote(dv_x.at[0], dv_x.at[1], xpeer)
    da = nt(dqk[:, :576], w5[0]) + nt(dqk[:, 576:], w1[0]) + nt(dvb, w1[1])
    gain1 = jnp.sum(da * normed, axis=0, keepdims=True)
    gg_out[...] = jnp.concatenate([gain1, gain2, jnp.zeros((6, gain1.shape[1]), F32)], axis=0)
    gg_copy = remote(gg_out, gg_in, xpeer)
    f = da * attn_g
    gin_ref[...] = dm1 + rr * (f - normed * jnp.mean(f * normed, axis=-1, keepdims=True))
    slots[0] = ag_z(0)
    for c in (a_copy, t_copy, dm_copy, dqk_copy, dv_copy):
        c.wait_recv()
    a_all = jnp.concatenate([a_half[0], a_half[2]], axis=0)
    t_all = jnp.concatenate([t_half[0], t_half[2]], axis=0)
    gw_o = tn(t_all, jnp.concatenate([dm_x[0], dm_x[1]], axis=0)).astype(BF16)
    gw_qk = tn(a_all, jnp.concatenate([dqk_x[0], dqk_x[1]], axis=0)).astype(BF16)
    gw_v = tn(a_all, jnp.concatenate([dv_x[0], dv_x[1]], axis=0)).astype(BF16)
    columns = [
        gw_qk[:, :384], gw_qk[:, 384:], gw_o[:, :384],
        jnp.concatenate([gw_o[:, 384:], gw_v], axis=1),
    ]
    gg_copy.wait_recv()
    gg = pick(gg_out[...] + gg_in[...], s)
    gg = jnp.concatenate([gg, jnp.zeros((8, 384 - dm), F32)], axis=1)
    row32 = lax.broadcasted_iota(jnp.int32, (32, 384), 0)
    for cc in range(4):
        for r in range(3):
            g3[r * 4 + cc] = columns[cc][r * 80 : (r + 1) * 80]
        g3[12 + cc, 0:48] = columns[cc][240:288]
        if cc < 2:
            tail = jnp.where(row32 == 0, jnp.broadcast_to(gg[cc : cc + 1], (32, 384)), 0.0)
        else:
            tail = jnp.zeros((32, 384), F32)
        g3[12 + cc, 48:80] = tail.astype(BF16)
    rs_core(2)
    slots[1] = ag_z(1)
    rs_y(2)
    ag_y(0)
    rs_z(2)
    slots[2] = ag_z(2)
    ag_y(1)
    ag_core(0)
    ag_y(2)
    ag_core(1)
    ag_core(2)
    for st in state:
        st.wait_recv()
    for c in started:
        c.wait_send()


def unpack_kernel(
    b_hbm, i_hbm, o1_hbm, o2_hbm, o3_hbm,
    block_ref, gin_ref, ag_ref, q_ref, k_ref, v_ref, o_ref, fg_ref, gate_ref, up_ref, down_ref,
    b_ref, i_ref, o1_ref, o2_ref, o3_ref, sem,
):
    pairs = (
        (b_hbm, b_ref), (i_hbm, i_ref), (o1_hbm, o1_ref), (o2_hbm, o2_ref), (o3_hbm, o3_ref),
    )
    copies = [pltpu.make_async_copy(src, dst, sem.at[i]) for i, (src, dst) in enumerate(pairs)]
    for c in copies:
        c.start()
    copies[0].wait()
    block_ref[...] = b_ref[...].T
    copies[1].wait()
    gin_ref[...] = i_ref[...].T
    copies[2].wait()
    half = ag_ref.shape[1]
    ffh = gate_ref.shape[2] // 2
    for f in range(2):
        for yy in range(2):
            for t, ref in enumerate((gate_ref, up_ref)):
                for zz in range(2):
                    lo = f * ffh + zz * 384
                    ref[0, yy * 144 : (yy + 1) * 144, lo : lo + 384] = o1_ref[
                        f * 8 + yy * 4 + t * 2 + zz
                    ].astype(F32)
    copies[3].wait()
    down_ref[0] = o2_ref[...].reshape(down_ref.shape[1:]).astype(F32)
    copies[4].wait()
    for r in range(4):
        lo = r * 80
        n = 80 if r < 3 else 48
        rows = slice(lo, lo + n)
        q_ref[0, rows, :384] = o3_ref[r * 4, :n].astype(F32)
        mid = o3_ref[r * 4 + 1, :n].astype(F32)
        q_ref[0, rows, 384:] = mid[:, :192]
        k_ref[0, rows] = mid[:, 192:]
        o_ref[0, rows, :384] = o3_ref[r * 4 + 2, :n].astype(F32)
        last = o3_ref[r * 4 + 3, :n].astype(F32)
        o_ref[0, rows, 384:] = last[:, :192]
        v_ref[0, rows] = last[:, 192:]
    ag_ref[...] = o3_ref[12, 48:64].astype(F32)[0:1, :half]
    fg_ref[...] = o3_ref[13, 48:64].astype(F32)[0:1, :half]


def fused_body(
    tokens, block_order, attn_gain, q_weight, k_weight, v_weight, o_weight, ffn_gain,
    gate_weight, up_weight, down_weight, cotangent,
):
    rows, width = tokens.shape
    half = attn_gain.shape[1]
    ff = gate_weight.shape[2]
    vm = pl.BlockSpec(memory_space=pltpu.VMEM)
    hbm = pl.BlockSpec(memory_space=pl.ANY)
    shapes = [(144, 384), (48, width), (80, 384)]

    def buf(*shape, dtype=BF16):
        return pltpu.VMEM(shape, dtype)

    scratch = [
        buf(width, rows), buf(width, rows), buf(rows, width), buf(width, ff // 2),
        buf(2, width, width),
        buf(2, width, KV * HD), buf(width, ff // 2), buf(width, ff // 2),
        buf(8, width, dtype=F32), buf(8, width, dtype=F32),
        buf(rows, width), buf(2, rows, 384), buf(2 * rows, width), buf(rows, width),
        buf(rows, width), buf(rows, width), buf(rows, width),
        buf(KV, 3 * rows, 2 * rows, dtype=F32), buf(3, rows, half), buf(3, rows, half),
        buf(2, rows, width), buf(rows, 384), buf(rows, 384), buf(2, rows, 768),
        buf(2, rows, 192), buf(8, width, dtype=F32), buf(8, width, dtype=F32),
    ]
    for count in (16, 8, 4, 3, 2):
        scratch += [buf(count, *sh) for sh in shapes]
    scratch += [
        pltpu.SemaphoreType.DMA((64,)), pltpu.SemaphoreType.DMA((64,)),
        pltpu.SemaphoreType.DMA((9,)),
    ]
    block_out, input_grad, o1, o2, o3 = pl.pallas_call(
        fused_kernel,
        out_shape=(
            jax.ShapeDtypeStruct((rows, width), F32),
            jax.ShapeDtypeStruct((rows, width), F32),
            *[jax.ShapeDtypeStruct((16, *sh), BF16) for sh in shapes],
        ),
        in_specs=[
            hbm, pl.BlockSpec(memory_space=pltpu.SMEM), vm, *[hbm] * 4, vm, *[hbm] * 4,
        ],
        out_specs=[vm] * 5,
        scratch_shapes=scratch,
        compiler_params=pltpu.CompilerParams(
            collective_id=0, has_side_effects=True, vmem_limit_bytes=56 * 1024 * 1024
        ),
    )(
        tokens.T, block_order, attn_gain, q_weight, k_weight, v_weight, o_weight, ffn_gain,
        gate_weight, up_weight, down_weight[0].T, cotangent.T,
    )
    out_shapes = [
        (width, rows), (width, rows), (1, half), (1, half, width), (1, half, KV * HD),
        (1, half, KV * HD), (1, half, width), (1, half), (1, half, ff), (1, half, ff),
        (1, ff // 2, width),
    ]
    out = pl.pallas_call(
        unpack_kernel,
        out_shape=tuple(jax.ShapeDtypeStruct(shape, F32) for shape in out_shapes),
        in_specs=[hbm] * 5,
        out_specs=(vm,) * 11,
        scratch_shapes=[
            buf(rows, width, dtype=F32), buf(rows, width, dtype=F32),
            *[buf(16, *sh) for sh in shapes], pltpu.SemaphoreType.DMA((5,)),
        ],
        compiler_params=pltpu.CompilerParams(vmem_limit_bytes=40 * 1024 * 1024),
    )(block_out, input_grad, o1, o2, o3)
    return (out[0].T, out[1].T, *out[2:])


def solution(mesh):
    placed = (
        P(("rep", "shard"), None),
        P("rep", None),
        P(None, "shard"),
        P(None, "shard", None),
        P(None, "shard", None),
        P(None, "shard", None),
        P(None, "shard", None),
        P(None, "shard"),
        P(None, "shard", None),
        P(None, "shard", None),
        P(None, "shard", None),
        P(("rep", "shard"), None),
    )
    fused = mesh.shape["shard"] == 2 and mesh.shape["rep"] == 16
    return jax.shard_map(
        fused_body if fused else body,
        mesh=mesh,
        in_specs=placed,
        out_specs=(
            P(("rep", "shard"), None),
            P(("rep", "shard"), None),
            P(None, "shard"),
            P(None, "shard", None),
            P(None, "shard", None),
            P(None, "shard", None),
            P(None, "shard", None),
            P(None, "shard"),
            P(None, "shard", None),
            P(None, "shard", None),
            P(None, "shard", None),
        ),
        check_vma=False,
    )
```
